256 devices in a mesh: seq: 32 (over z, y), mp: 8 (over x, core).
Axes of the slice: x: 4, y: 4, z: 8, core: 2. Of those that a mesh axis runs over, the one named last changes fastest.
Arguments:
- tokens: bfloat16 [49152, 2048], P('seq', 'mp'), may hold values from -12 to 12
- cluster_ids: int32 [49152, 1], P('seq'), may hold values from 0 to 63, as said below
- w_query: bfloat16 [2048, 2048], P(None, 'mp'), may hold values from -0.125 to 0.125
- w_value: bfloat16 [2048, 2048], P(None, 'mp'), may hold values from -0.125 to 0.125
- w_out: bfloat16 [2048, 2048], P('mp'), may hold values from -0.125 to 0.125
Outputs:
- mixed: bfloat16 [49152, 2048], P('seq', 'mp')
The draws below stay inside these ranges and needn't reach their ends.
Inputs may be any that keep to these rules, and one draw needn't show every extreme that they name: `cluster_ids`: in the rows of one index of seq, no cluster holds more than 48 tokens, and some cluster holds exactly 48.
All inputs are finite; a program needn't handle non-finite values.
Results may differ from the reference program's by a relative error of at most 0.0062.
Values may be sent and summed in bfloat16 or wider, within the bound.
A program may use at most 128 MiB of HBM per device.

```python
import jax
import jax.numpy as jnp
from jax import lax

D = 2048
HEADS = 16
HD = 128
TOK_DEV = 1536
TOKENS = 49152
CLUSTERS = 64
CAP = 48


def shared_ids(key):
    devices = TOKENS // TOK_DEV
    per = TOK_DEV // CLUSTERS
    pair_key, count_key, order_key = jax.random.split(jax.random.fold_in(key, 11), 3)
    pairing = jax.random.permutation(pair_key, CLUSTERS).astype(jnp.int32)
    heavy = pairing[0::2]
    light = pairing[1::2]
    spill = jax.random.randint(count_key, (devices, CLUSTERS // 2), 0, max(per // 2, 1) + 1).astype(jnp.int32)
    spill = spill.at[:, 0].set(0)
    slot = jnp.arange(2 * per, dtype=jnp.int32)
    labels = jnp.where(slot[None, None, :] < (2 * per - spill)[:, :, None], heavy[None, :, None], light[None, :, None])
    labels = labels.reshape(devices, TOK_DEV).astype(jnp.int32)
    orders = jax.vmap(lambda one_key: jax.random.permutation(one_key, TOK_DEV))(jax.random.split(order_key, devices))
    shuffled = jnp.take_along_axis(labels, orders.astype(jnp.int32), axis=1)
    return shuffled.reshape(TOKENS).astype(jnp.int32)


def draw_cluster_ids(key, part):
    ids = shared_ids(key)
    return ids[:, None]


def draw_tokens(key, part):
    ids = shared_ids(key)
    key = jax.random.fold_in(key, 7)
    proto_key, pick_key, noise_key = jax.random.split(key, 3)
    choose = jax.random.randint(pick_key, (TOKENS,), 0, 4).astype(jnp.int32)
    protos = jnp.clip(jax.random.normal(proto_key, (CLUSTERS, 4, D), jnp.float32), -3.5, 3.5)
    noise = 0.5 * jnp.clip(jax.random.normal(noise_key, (TOKENS, D), jnp.float32), -3.0, 3.0)
    rows = protos[ids, choose]
    return jnp.clip(rows + noise, -12.0, 12.0).astype(jnp.bfloat16)


def steps_of(rng, shape, shards, least, top_value):
    factor_of = 1.0
    for position, blocks in shards:
        draws = jax.random.uniform(jax.random.fold_in(jax.random.fold_in(rng, 6), position), (blocks,), jnp.float32, least / len(shards), top_value / len(shards))
        factor_of = factor_of * jnp.repeat(jnp.exp(draws), shape[position] // blocks).reshape((-1,) + (1,) * (len(shape) - 1 - position))
    return factor_of


def normal_values(stream_key, dims, scale, bound, shards=(), held_as=jnp.bfloat16):
    level = steps_of(stream_key, dims, shards, -0.22, 0.18) if shards else 1.0
    drawn = jax.random.normal(stream_key, dims, jnp.float32) * scale * level
    return jnp.minimum(jnp.maximum(drawn, -bound), bound).astype(held_as)


def setup_inputs(seed: int = 0) -> dict:
    streams_of = jax.random.split(jax.random.key(seed), 6)
    tokens = draw_tokens(jax.random.fold_in(streams_of[5], 71), 0)
    cluster_ids = draw_cluster_ids(jax.random.fold_in(streams_of[5], 71), 0)
    w_query = normal_values(streams_of[2], (D, HEADS * HD), D ** -0.5, 0.125, ((1, 8),))
    w_value = normal_values(streams_of[3], (D, HEADS * HD), D ** -0.5, 0.125, ((1, 8),))
    w_out = normal_values(streams_of[4], (HEADS * HD, D), (HEADS * HD) ** -0.5, 0.125, ((0, 8),))
    return dict(tokens=tokens, cluster_ids=cluster_ids, w_query=w_query, w_value=w_value, w_out=w_out)


far_position = 1073741824

def reference(tokens, cluster_ids, w_query, w_value, w_out):
    query = jnp.dot(tokens, w_query, preferred_element_type=jnp.float32).astype(jnp.bfloat16)
    value = jnp.dot(tokens, w_value, preferred_element_type=jnp.float32).astype(jnp.bfloat16)
    sources = TOKENS // TOK_DEV
    ids = cluster_ids[:, 0].reshape(sources, TOK_DEV)
    onehot = (ids[:, :, None] == jnp.arange(CLUSTERS, dtype=jnp.int32)[None, None, :]).astype(jnp.int32)
    ranks = jnp.cumsum(onehot, axis=1) - onehot
    slots = lax.optimization_barrier(jnp.sum(ranks * onehot, axis=2)).astype(jnp.int32)
    dest = (ids * CAP + slots).astype(jnp.int32)
    token_index = jnp.arange(TOKENS, dtype=jnp.int32).reshape(sources, TOK_DEV)
    source_index = jnp.broadcast_to(jnp.arange(sources, dtype=jnp.int32)[:, None], (sources, TOK_DEV))
    table = jnp.full((sources, CLUSTERS * CAP), -1, jnp.int32).at[source_index, dest].set(token_index)
    table = table.reshape(sources, CLUSTERS, CAP).transpose(1, 0, 2).reshape(CLUSTERS, sources * CAP)

    def one_cluster(index_row):
        valid = index_row >= 0
        safe = jnp.maximum(index_row, 0).astype(jnp.int32)
        keep = valid[:, None].astype(jnp.bfloat16)
        qrows = (query[safe] * keep).reshape(-1, HEADS, HD).astype(jnp.float32)
        vrows = (value[safe] * keep).reshape(-1, HEADS, HD).astype(jnp.float32)
        positions = jnp.where(valid, safe, far_position)
        scores = jnp.einsum('sha,tha->hst', qrows, qrows) / jnp.sqrt(jnp.float32(HD))
        allowed = positions[None, :] <= positions[:, None]
        scores = jnp.where(allowed[None], scores, jnp.float32(-1e+30))
        top = lax.optimization_barrier(jnp.max(scores, axis=2, keepdims=True))
        expo = jnp.exp(scores - top)
        weights = (expo / lax.optimization_barrier(jnp.sum(expo, axis=2, keepdims=True))).astype(jnp.bfloat16)
        attended = jnp.einsum('hst,tha->sha', weights.astype(jnp.float32), vrows)
        return attended.astype(jnp.bfloat16).reshape(-1, HEADS * HD)
    results = lax.map(one_cluster, table).reshape(CLUSTERS * sources * CAP, HEADS * HD)
    where_flat = (ids * (sources * CAP) + source_index * CAP + slots).reshape(-1).astype(jnp.int32)
    attended = results[where_flat]
    return jnp.dot(attended, w_out, preferred_element_type=jnp.float32).astype(jnp.bfloat16)
```

```python
import functools

import jax
import jax.numpy as jnp
import numpy as np
from jax import lax
from jax.experimental import pallas as pl
from jax.experimental.pallas import tpu as pltpu
from jax.sharding import PartitionSpec as P

HD = 128
CAP = 48
NZ, NY, NX = 8, 4, 4
NSEQ = NZ * NY
NEG = -1e30
MESH = pl.DeviceIdType.MESH
BF = jnp.bfloat16
F32 = jnp.float32


def peer_of(s, r, sign):
    g, hi, dy = r // 8, (r // 4) % 2, r % 4
    minus = jnp.where(g == 0, 4, NZ - g)
    dz = jnp.where(hi == 0, g, minus)
    z, y = s // NY, s % NY
    return ((z + sign * dz + NZ) % NZ) * NY + (y + sign * dy + NY) % NY


def slot_base(ids, s):
    z, y = s // NY, s % NY
    owner, o = ids >> 1, ids & 1
    dz = ((owner >> 2) - z) & (NZ - 1)
    dy = ((owner & 3) - y) & (NY - 1)
    hi = dz >> 2
    g = jnp.where(hi == 1, (NZ - dz) & 3, dz)
    r = g * 8 + hi * 4 + dy
    return (o * NSEQ + r) * CAP


def greet(peers_seq, peers_mp, s, m):
    barrier = pltpu.get_barrier_semaphore()

    def hello(r, carry):
        pl.semaphore_signal(
            barrier, inc=1, device_id=(peer_of(s, r, 1), m), device_id_type=MESH
        )
        return carry

    lax.fori_loop(1, NSEQ, hello, 0)
    for peer in peers_mp:
        pl.semaphore_signal(barrier, inc=1, device_id=(s, peer), device_id_type=MESH)
    pl.semaphore_wait(barrier, NSEQ - 1 + len(peers_mp))


class Ring:
    def __init__(self, G, place, nch, s, m, ssem, rsem):
        self.G, self.place, self.nch = G, place, nch
        self.s, self.m, self.ssem, self.rsem = s, m, ssem, rsem
        self.rows = G.shape[2]
        x, c = m // 2, m % 2
        self.right = ((x + 1) % NX) * 2 + c
        self.left = ((x + NX - 1) % NX) * 2 + c
        self.far = ((x + 2) % NX) * 2 + c
        self.sib = x * 2 + 1 - c

    def _copy(self, kind, k, block, to, half=None):
        p = self.place(k)
        ref = self.G.at[block, p]
        if half is not None:
            h = self.rows // 2
            ref = self.G.at[block, p, pl.ds(half * h, h)]
        return pltpu.make_async_remote_copy(
            src_ref=ref,
            dst_ref=ref,
            send_sem=self.ssem.at[kind, k],
            recv_sem=self.rsem.at[kind, k],
            device_id=(self.s, to),
            device_id_type=MESH,
        )

    def sib_of(self, block):
        return (block // 2) * 2 + 1 - block % 2

    def send(self, i, k):
        block, to, half = (
            (self.m, self.right, None),
            (self.m, self.left, None),
            (self.m, self.sib, None),
            (self.left, self.right, 0),
            (self.right, self.left, 1),
            (self.left, self.sib, None),
            (self.right, self.sib, None),
            (self.far, self.sib, None),
        )[i]
        return self._copy(i, k, block, to, half)

    def arrival(self, i, k):
        block, to, half = (
            (self.left, self.right, None),
            (self.right, self.left, None),
            (self.sib, self.sib, None),
            (self.far, self.right, 0),
            (self.far, self.left, 1),
            (self.sib_of(self.left), self.sib, None),
            (self.sib_of(self.right), self.sib, None),
            (self.sib_of(self.far), self.sib, None),
        )[i]
        return self._copy(i, k, block, to, half)

    def stage(self, which, k):
        if which == 0:
            for i in (0, 1, 2):
                self.send(i, k).start()
        elif which == 1:
            self.arrival(0, k).wait_recv()
            self.send(3, k).start()
            self.send(5, k).start()
            self.arrival(1, k).wait_recv()
            self.send(4, k).start()
            self.send(6, k).start()
        elif which == 2:
            self.arrival(3, k).wait_recv()
            self.arrival(4, k).wait_recv()
            self.send(7, k).start()
        else:
            for i in (2, 5, 6, 7):
                self.arrival(i, k).wait_recv()

    def run(self, ready, compute):
        n = self.nch

        def step(t, carry):
            @pl.when(t < n)
            def _():
                ready(t)
                self.stage(0, t)

            @pl.when((t >= 1) & (t < n + 1))
            def _():
                self.stage(1, t - 1)

            @pl.when((t >= 2) & (t < n + 2))
            def _():
                self.stage(2, t - 2)

            @pl.when(t >= 3)
            def _():
                self.stage(3, t - 3)
                compute(t - 3)

            return carry

        lax.fori_loop(0, n + 3, step, 0)

        def drain(k, carry):
            for i in range(8):
                self.send(i, k).wait_send()
            return carry

        lax.fori_loop(0, n, drain, 0)


def dispatch_kernel(
    tok_ref, ids_ref, wq_ref, wv_ref, wo_ref,
    q_ref, v_ref, bias_ref, wcol_ref,
    buf, G, cnt, dest, onehot,
    ssem, rsem, dsend, drecv, csend, crecv, wsend, wrecv,
):
    s, m = lax.axis_index("seq"), lax.axis_index("mp")
    tok = tok_ref.shape[0]
    greet(None, [lax.rem(m + i, 8) for i in range(1, 8)], s, m)

    def wcopy(i, block, to):
        return pltpu.make_async_remote_copy(
            src_ref=wo_ref.at[:, pl.ds(pl.multiple_of(to * 256, 256), 256)],
            dst_ref=wcol_ref.at[block],
            send_sem=wsend.at[i],
            recv_sem=wrecv.at[i],
            device_id=(s, to),
            device_id_type=MESH,
        )

    ids = ids_ref[...]
    cl = lax.broadcasted_iota(jnp.int32, (128, tok), 0)
    onehot[...] = (cl == ids).astype(F32).astype(BF)
    upper = (
        lax.broadcasted_iota(jnp.int32, (256, 256), 0)
        < lax.broadcasted_iota(jnp.int32, (256, 256), 1)
    ).astype(F32).astype(BF)
    seen = jnp.zeros((128, 1), F32)
    for b in range(tok // 256):
        part = onehot[:, b * 256:(b + 1) * 256]
        wide = part.astype(F32)
        ahead = jnp.dot(part, upper, preferred_element_type=F32) + seen
        slot = jnp.sum(ahead * wide, axis=0, keepdims=True)
        base = slot_base(ids[:, b * 256:(b + 1) * 256], s)
        dest[:, b * 256:(b + 1) * 256] = base + slot.astype(jnp.int32)
        seen = seen + jnp.sum(wide, axis=1, keepdims=True)
    cnt[0] = lax.dot_general(
        jnp.ones((8, tok), BF), onehot[...], (((1,), (1,)), ((), ())),
        preferred_element_type=F32,
    )

    def block_copy(o, r):
        g, j = r // 8, r % 8
        return pltpu.make_async_remote_copy(
            src_ref=buf.at[o * 4 + g, pl.ds(pl.multiple_of(j * CAP, CAP), CAP)],
            dst_ref=G.at[m, o * 4 + g, pl.ds(pl.multiple_of(j * CAP, CAP), CAP)],
            send_sem=dsend.at[o * 4 + g],
            recv_sem=drecv.at[o * 4 + g],
            device_id=(peer_of(s, r, 1), m),
            device_id_type=MESH,
        )

    def count_copy(r):
        return pltpu.make_async_remote_copy(
            src_ref=cnt.at[0],
            dst_ref=cnt.at[r],
            send_sem=csend,
            recv_sem=crecv,
            device_id=(peer_of(s, r, 1), m),
            device_id_type=MESH,
        )

    def place(k):
        return (k // 4) * 4 + (k + 1) % 4

    def scatter(k, carry):
        p = place(k)
        o, g = p // 4, p % 4
        row = lax.broadcasted_iota(jnp.int32, (8 * CAP, tok), 0) + p * (8 * CAP)
        pick = (row == dest[...]).astype(F32).astype(BF)
        rows = jnp.dot(pick, tok_ref[...], preferred_element_type=F32).astype(BF)
        buf[p] = rows

        @pl.when(g == 0)
        def _():
            G[m, p, 0:CAP] = rows[0:CAP]

        def send(j, c2):
            block_copy(o, g * 8 + j).start()
            return c2

        lax.fori_loop(jnp.where(g == 0, 1, 0), 8, send, 0)
        return carry

    lax.fori_loop(0, 8, scatter, 0)
    for i in range(1, 8):
        wcopy(i, m, lax.rem(m + i, 8)).start()
    wcol_ref[m] = wo_ref[:, pl.ds(pl.multiple_of(m * 256, 256), 256)]

    def send_count(r, carry):
        count_copy(r).start()
        return carry

    lax.fori_loop(1, NSEQ, send_count, 0)

    def whole(ref, sem_s, sem_r):
        return pltpu.make_async_remote_copy(
            src_ref=ref, dst_ref=ref, send_sem=sem_s, recv_sem=sem_r,
            device_id=(s, m), device_id_type=MESH,
        )

    def ready(k):
        p = place(k)

        @pl.when(p % 4 == 0)
        def _():
            whole(G.at[m, p, pl.ds(CAP, 7 * CAP)], dsend.at[p], drecv.at[p]).wait_recv()

        @pl.when(p % 4 != 0)
        def _():
            whole(G.at[m, p], dsend.at[p], drecv.at[p]).wait_recv()

    def project(k):
        p = place(k)
        o, g = p // 4, p % 4
        rows = jnp.concatenate([G[i, p] for i in range(8)], axis=1)
        for w_ref, out_ref in ((wq_ref, q_ref), (wv_ref, v_ref)):
            got = jnp.dot(rows, w_ref[...], preferred_element_type=F32).astype(BF)
            for j in range(8):
                src = peer_of(s, g * 8 + j, -1)
                out_ref[o, pl.ds(pl.multiple_of(src * CAP, CAP), CAP)] = got[j * CAP:(j + 1) * CAP]

    ring = Ring(G, place, 8, s, m, ssem, rsem)
    ring.run(ready, project)

    whole(cnt.at[pl.ds(1, NSEQ - 1)], csend, crecv).wait_recv()
    lane = lax.broadcasted_iota(jnp.int32, (NSEQ, 128), 1)
    r = lax.broadcasted_iota(jnp.int32, (NSEQ, tok), 0)
    g, hi, dy = r >> 3, (r >> 2) & 1, r & 3
    dz = jnp.where(hi == 0, g, jnp.where(g == 0, 4, NZ - g))
    src = (((s // NY) - dz) & (NZ - 1)) * NY + (((s % NY) - dy) & (NY - 1))
    off = lax.broadcasted_iota(jnp.int32, (NSEQ, tok), 1) - src * CAP
    tall = cnt[:, 0, :]
    for o in range(2):
        have = jnp.sum(jnp.where(lane == 2 * s + o, tall, 0.0), axis=1, keepdims=True)
        held = jnp.where((off >= 0) & (off.astype(F32) < have), 1.0, 0.0)
        held = jnp.sum(held, axis=0, keepdims=True)
        bias_ref[o] = jnp.broadcast_to((1.0 - held) * NEG, (8, tok))

    for i in range(1, 8):
        one = wcopy(i, lax.rem(m + 8 - i, 8), lax.rem(m + i, 8))
        one.wait_recv()
        one.wait_send()
    whole(cnt.at[pl.ds(1, NSEQ - 1)], csend, crecv).wait_send()

    def done(p, carry):
        @pl.when(p % 4 == 0)
        def _():
            whole(buf.at[p, pl.ds(CAP, 7 * CAP)], dsend.at[p], drecv.at[p]).wait_send()

        @pl.when(p % 4 != 0)
        def _():
            whole(buf.at[p], dsend.at[p], drecv.at[p]).wait_send()

        return carry

    lax.fori_loop(0, 8, done, 0)


def attend_kernel(q_ref, v_ref, bias_ref, out_ref, *, block):
    span = q_ref.shape[1]
    fold = np.float32(1.4426950408889634 / np.sqrt(128.0))
    ones = jnp.ones((span, HD), BF)
    v = jnp.concatenate([v_ref[0], ones], axis=1)
    keys = q_ref[0]
    below = (
        lax.broadcasted_iota(jnp.int32, (block, block), 0)
        >= lax.broadcasted_iota(jnp.int32, (block, block), 1)
    )
    for i in range(span // block):
        lo, hi = i * block, (i + 1) * block
        q = keys[lo:hi]
        dims = (((1,), (1,)), ((), ()))
        bias = bias_ref[0, 0:1, :]
        sd = lax.dot_general(q, keys[lo:hi], dims, preferred_element_type=F32) * fold
        sd = jnp.where(below, sd + bias[:, lo:hi], NEG)
        if i:
            sl = lax.dot_general(q, keys[:lo], dims, preferred_element_type=F32) * fold
            scores = jnp.concatenate([sl + bias[:, :lo], sd], axis=1)
        else:
            scores = sd
        top = jnp.max(scores, axis=1, keepdims=True)
        expo = jnp.exp2(scores - top).astype(BF)
        got = jnp.dot(expo, v[:hi], preferred_element_type=F32)
        out_ref[0, lo:hi] = (got[:, :HD] / got[:, HD:HD + 1]).astype(BF)


def return_kernel(
    att_ref, ids_ref, wcol_ref, out_ref, back, G, dest, ssem, rsem, bsend, brecv
):
    s, m = lax.axis_index("seq"), lax.axis_index("mp")
    tok = ids_ref.shape[0]
    chunk = G.shape[2]
    ring = Ring(G, lambda k: k, tok // chunk, s, m, ssem, rsem)
    greet(None, [ring.left, ring.right, ring.sib], s, m)

    def back_copy(o, r):
        src = peer_of(s, r, -1)
        return pltpu.make_async_remote_copy(
            src_ref=att_ref.at[o, pl.ds(pl.multiple_of(src * CAP, CAP), CAP)],
            dst_ref=back.at[o, pl.ds(pl.multiple_of(r * CAP, CAP), CAP)],
            send_sem=bsend.at[o],
            recv_sem=brecv.at[o],
            device_id=(src, m),
            device_id_type=MESH,
        )

    for o in range(2):
        def send(r, carry):
            back_copy(o, r).start()
            return carry

        lax.fori_loop(1, NSEQ, send, 0)
        back[o, 0:CAP] = att_ref[o, pl.ds(pl.multiple_of(s * CAP, CAP), CAP)]

    ids = ids_ref[...]
    cl = lax.broadcasted_iota(jnp.int32, (256, 128), 1)
    lower = (
        lax.broadcasted_iota(jnp.int32, (256, 256), 1)
        < lax.broadcasted_iota(jnp.int32, (256, 256), 0)
    ).astype(F32).astype(BF)
    seen = jnp.zeros((1, 128), F32)
    for b in range(tok // 256):
        wide = (cl == ids[b * 256:(b + 1) * 256]).astype(F32)
        ahead = jnp.dot(lower, wide.astype(BF), preferred_element_type=F32) + seen
        slot = jnp.sum(ahead * wide, axis=1, keepdims=True)
        dest[b * 256:(b + 1) * 256, :] = slot_base(ids[b * 256:(b + 1) * 256], s) + slot.astype(jnp.int32)
        seen = seen + jnp.sum(wide, axis=0, keepdims=True)

    def whole(o):
        ref = back.at[o, pl.ds(CAP, (NSEQ - 1) * CAP)]
        return pltpu.make_async_remote_copy(
            src_ref=ref, dst_ref=ref, send_sem=bsend.at[o], recv_sem=brecv.at[o],
            device_id=(s, m), device_id_type=MESH,
        )

    for o in range(2):
        whole(o).wait_recv()

    def ready(k):
        at = dest[pl.ds(pl.multiple_of(k * chunk, chunk), chunk), :]
        got = jnp.zeros((chunk, 256), F32)
        for o in range(2):
            col = lax.broadcasted_iota(jnp.int32, (chunk, tok), 1) + o * tok
            pick = (col == at).astype(F32).astype(BF)
            got = got + jnp.dot(pick, back[o], preferred_element_type=F32)
        G[m, k] = got.astype(BF)

    def project(k):
        rows = jnp.concatenate([G[i, k] for i in range(8)], axis=1)
        w = wcol_ref[...].reshape(2048, 256)
        got = jnp.dot(rows, w, preferred_element_type=F32)
        out_ref[pl.ds(pl.multiple_of(k * chunk, chunk), chunk)] = got.astype(BF)

    ring.run(ready, project)
    for o in range(2):
        whole(o).wait_send()


def params(cid):
    return pltpu.CompilerParams(
        collective_id=cid, has_side_effects=True, vmem_limit_bytes=56 * 1024 * 1024
    )


def shards(tokens, cluster_ids, w_query, w_value, w_out):
    tok = tokens.shape[0]
    vmem = pl.BlockSpec(memory_space=pltpu.VMEM)
    dma = pltpu.SemaphoreType.DMA
    q, v, bias, wcol = pl.pallas_call(
        dispatch_kernel,
        out_shape=[
            jax.ShapeDtypeStruct((2, tok, 256), BF),
            jax.ShapeDtypeStruct((2, tok, 256), BF),
            jax.ShapeDtypeStruct((2, 8, tok), F32),
            jax.ShapeDtypeStruct((8, 256, 256), BF),
        ],
        in_specs=[vmem] * 5,
        out_specs=[vmem] * 4,
        scratch_shapes=[
            pltpu.VMEM((8, 8 * CAP, 256), BF),
            pltpu.VMEM((8, 8, 8 * CAP, 256), BF),
            pltpu.VMEM((NSEQ, 8, 128), F32),
            pltpu.VMEM((1, tok), jnp.int32),
            pltpu.VMEM((128, tok), BF),
            dma((8, 8)), dma((8, 8)), dma((8,)), dma((8,)), dma, dma, dma((8,)), dma((8,)),
        ],
        compiler_params=params(1),
        name="dispatch",
    )(tokens, cluster_ids.reshape(1, tok), w_query, w_value, w_out)

    attended = pl.pallas_call(
        functools.partial(attend_kernel, block=256),
        grid=(2, 2),
        out_shape=jax.ShapeDtypeStruct((2, tok, 256), BF),
        in_specs=[
            pl.BlockSpec((1, tok, HD), lambda o, h: (o, 0, h)),
            pl.BlockSpec((1, tok, HD), lambda o, h: (o, 0, h)),
            pl.BlockSpec((1, 8, tok), lambda o, h: (o, 0, 0)),
        ],
        out_specs=pl.BlockSpec((1, tok, HD), lambda o, h: (o, 0, h)),
        compiler_params=pltpu.CompilerParams(vmem_limit_bytes=40 * 1024 * 1024),
        name="attend",
    )(q, v, bias)

    chunk = 256
    return pl.pallas_call(
        return_kernel,
        out_shape=jax.ShapeDtypeStruct((tok, 256), BF),
        in_specs=[vmem] * 3,
        out_specs=vmem,
        scratch_shapes=[
            pltpu.VMEM((2, tok, 256), BF),
            pltpu.VMEM((8, tok // chunk, chunk, 256), BF),
            pltpu.VMEM((tok, 1), jnp.int32),
            dma((8, tok // chunk)), dma((8, tok // chunk)), dma((2,)), dma((2,)),
        ],
        compiler_params=params(2),
        name="give_back",
    )(attended, cluster_ids, wcol)


def solution(mesh):
    return jax.shard_map(
        shards,
        mesh=mesh,
        in_specs=(P("seq", "mp"), P("seq", None), P(None, "mp"), P(None, "mp"), P("mp", None)),
        out_specs=P("seq", "mp"),
        check_vma=False,
    )
```

```python
import functools

import jax
import jax.numpy as jnp
import numpy as np
from jax import lax
from jax.experimental import pallas as pl
from jax.experimental.pallas import tpu as pltpu
from jax.sharding import PartitionSpec as P

HD = 128
CAP = 48
NZ, NY, NX = 8, 4, 4
NSEQ = NZ * NY
NMP = 2 * NX
TOK = 1536
GROUPS = 4
BLK = 256
NEG = -1e30
MESH = pl.DeviceIdType.MESH
BF = jnp.bfloat16
F32 = jnp.float32
I32 = jnp.int32
FOLD = np.float32(1.4426950408889634 / np.sqrt(128.0))


def peer_of(s, r, sign):
    g, hi, dy = r // 8, (r // 4) % 2, r % 4
    minus = jnp.where(g == 0, 4, NZ - g)
    dz = jnp.where(hi == 0, g, minus)
    z, y = s // NY, s % NY
    return ((z + sign * dz + NZ) % NZ) * NY + (y + sign * dy + NY) % NY


def rank_of(cluster):
    return (cluster & 1) * NSEQ + (cluster >> 1)


def first_row(rank, s, caps):
    z, y = s // NY, s % NY
    owner, o = rank & (NSEQ - 1), rank >> 5
    dz = ((owner >> 2) - z) & (NZ - 1)
    dy = ((owner & 3) - y) & (NY - 1)
    hi = dz >> 2
    g = jnp.where(hi == 1, (NZ - dz) & 3, dz)
    r = g * 8 + hi * 4 + dy
    return jnp.where(o == 0, r * caps[0], NSEQ * caps[0] + r * caps[1])


class Ring:
    def __init__(self, chunks, s, m, ssem, rsem):
        self.chunks, self.s, self.m = chunks, s, m
        self.ssem, self.rsem = ssem, rsem
        x, c = m // 2, m % 2
        self.right = ((x + 1) % NX) * 2 + c
        self.left = ((x + NX - 1) % NX) * 2 + c
        self.far = ((x + 2) % NX) * 2 + c
        self.sib = x * 2 + 1 - c

    def _copy(self, kind, k, block, to, half=None):
        G, p = self.chunks[k]
        ref = G.at[block, p]
        if half is not None:
            h = G.shape[2] // 2
            ref = G.at[block, p, pl.ds(half * h, h)]
        return pltpu.make_async_remote_copy(
            src_ref=ref,
            dst_ref=ref,
            send_sem=self.ssem.at[kind, k],
            recv_sem=self.rsem.at[kind, k],
            device_id=(self.s, to),
            device_id_type=MESH,
        )

    def send(self, i, k):
        block, to, half = (
            (self.m, self.right, None),
            (self.m, self.left, None),
            (self.m, self.sib, None),
            (self.left, self.right, 0),
            (self.right, self.left, 1),
            (self.left, self.sib, None),
            (self.right, self.sib, None),
            (self.far, self.sib, None),
        )[i]
        return self._copy(i, k, block, to, half)

    def arrival(self, i, k):
        other = lambda block: (block // 2) * 2 + 1 - block % 2
        block, half = (
            (self.left, None),
            (self.right, None),
            (self.sib, None),
            (self.far, 0),
            (self.far, 1),
            (other(self.left), None),
            (other(self.right), None),
            (other(self.far), None),
        )[i]
        return self._copy(i, k, block, self.sib, half)

    def step(self, t, ready, compute):
        n = len(self.chunks)
        if t < n:
            ready(t)
            for i in (0, 1, 2):
                self.send(i, t).start()
        if 1 <= t <= n:
            k = t - 1
            self.arrival(0, k).wait_recv()
            self.send(3, k).start()
            self.send(5, k).start()
            self.arrival(1, k).wait_recv()
            self.send(4, k).start()
            self.send(6, k).start()
        if 2 <= t <= n + 1:
            k = t - 2
            self.arrival(3, k).wait_recv()
            self.arrival(4, k).wait_recv()
            self.send(7, k).start()
        if 3 <= t:
            k = t - 3
            for i in (2, 5, 6, 7):
                self.arrival(i, k).wait_recv()
            compute(k)

    def drain(self):
        for k in range(len(self.chunks)):
            for i in range(8):
                self.send(i, k).wait_send()


def layer_kernel(
    tok_ref, row_ref, col_ref, wq_hbm, wv_hbm, wo_hbm,
    out_ref,
    wq, wv, wo, wcol, buf0, buf1, G0, G1, q0, q1, v0, v1, bias0, bias1,
    att0, att1, back0, back1, G2, cnt, onehot, drow, dcol,
    lsem, ssem1, rsem1, ssem2, rsem2, dsend, drecv, csend, crecv,
    bsend, brecv, wsend, wrecv,
    *, caps,
):
    s, m = lax.axis_index("seq"), lax.axis_index("mp")
    bufs, Gs, qs, vs = (buf0, buf1), (G0, G1), (q0, q1), (v0, v1)
    biases, atts, backs = (bias0, bias1), (att0, att1), (back0, back1)
    spans = (NSEQ * caps[0], NSEQ * caps[1])

    loads = [
        pltpu.make_async_copy(a, b, lsem.at[i])
        for i, (a, b) in enumerate(((wq_hbm, wq), (wv_hbm, wv), (wo_hbm, wo)))
    ]
    for one in loads:
        one.start()

    barrier = pltpu.get_barrier_semaphore()

    def hello(r, carry):
        pl.semaphore_signal(
            barrier, inc=1, device_id=(peer_of(s, r, 1), m), device_id_type=MESH
        )
        return carry

    lax.fori_loop(1, NSEQ, hello, 0)
    for i in range(1, NMP):
        pl.semaphore_signal(
            barrier, inc=1, device_id=(s, lax.rem(m + i, NMP)), device_id_type=MESH
        )

    ids = row_ref[...]
    onehot[...] = (lax.broadcasted_iota(I32, (128, TOK), 0) == ids).astype(F32).astype(BF)
    i0 = lax.broadcasted_iota(I32, (BLK, BLK), 0)
    i1 = lax.broadcasted_iota(I32, (BLK, BLK), 1)
    upper = (i0 < i1).astype(F32).astype(BF)
    seen = first_row(rank_of(lax.broadcasted_iota(I32, (128, 1), 0)), s, caps).astype(F32)
    for b in range(TOK // BLK):
        part = onehot[:, b * BLK:(b + 1) * BLK]
        wide = part.astype(F32)
        ahead = jnp.dot(part, upper, preferred_element_type=F32) + seen
        drow[:, b * BLK:(b + 1) * BLK] = jnp.sum(ahead * wide, axis=0, keepdims=True).astype(I32)
        seen = seen + jnp.sum(wide, axis=1, keepdims=True)
    cnt[0] = lax.dot_general(
        jnp.ones((8, TOK), BF), onehot[...], (((1,), (1,)), ((), ())),
        preferred_element_type=F32,
    )
    pl.semaphore_wait(barrier, NSEQ - 1 + NMP - 1)

    def whole(ref, sem_s, sem_r):
        return pltpu.make_async_remote_copy(
            src_ref=ref, dst_ref=ref, send_sem=sem_s, recv_sem=sem_r,
            device_id=(s, m), device_id_type=MESH,
        )

    def block_copy(o, g, j):
        at = pl.ds(pl.multiple_of(j * caps[o], 16), caps[o])
        return pltpu.make_async_remote_copy(
            src_ref=bufs[o].at[g, at],
            dst_ref=Gs[o].at[m, g, at],
            send_sem=dsend.at[o * GROUPS + g],
            recv_sem=drecv.at[o * GROUPS + g],
            device_id=(peer_of(s, g * 8 + j, 1), m),
            device_id_type=MESH,
        )

    def landed(o, g, ref):
        if g == 0:
            ref = ref.at[pl.ds(caps[o], 7 * caps[o])]
        return whole(ref, dsend.at[o * GROUPS + g], drecv.at[o * GROUPS + g])

    def scatter(o, g):
        n = 8 * caps[o]
        base = o * spans[0] + g * n
        row = lax.broadcasted_iota(I32, (n, TOK), 0) + base
        pick = (row == drow[...]).astype(F32).astype(BF)
        rows = jnp.dot(pick, tok_ref[...], preferred_element_type=F32).astype(BF)
        bufs[o][g] = rows
        if g == 0:
            Gs[o][m, 0, 0:caps[o]] = rows[0:caps[o]]

        def send(j, carry):
            block_copy(o, g, j).start()
            return carry

        lax.fori_loop(1 if g == 0 else 0, 8, send, 0)

    order = [(o, g) for o in range(2) for g in (1, 2, 3, 0)]
    for o, g in order[:GROUPS]:
        scatter(o, g)

    def count_copy(r):
        return pltpu.make_async_remote_copy(
            src_ref=cnt.at[0], dst_ref=cnt.at[r], send_sem=csend, recv_sem=crecv,
            device_id=(peer_of(s, r, 1), m), device_id_type=MESH,
        )

    def send_count(r, carry):
        count_copy(r).start()
        return carry

    def ready(t):
        o, g = order[t]
        landed(o, g, Gs[o].at[m, g]).wait_recv()

    def project(k):
        o, g = order[k]
        if k == 0:
            loads[0].wait()
            loads[1].wait()
            for o2 in range(2):
                for h in range(2):
                    vs[o2][:, h * 256 + HD:(h + 1) * 256] = jnp.ones((spans[o2], HD), BF)
        cap = caps[o]
        rows = jnp.concatenate([Gs[o][i, g] for i in range(NMP)], axis=1)
        query = jnp.dot(rows, wq[...], preferred_element_type=F32).astype(BF)
        value = jnp.dot(rows, wv[...], preferred_element_type=F32).astype(BF)
        for j in range(8):
            at = pl.ds(pl.multiple_of(peer_of(s, g * 8 + j, -1) * cap, 16), cap)
            qs[o][at] = query[j * cap:(j + 1) * cap]
            for h in range(2):
                vs[o][at, h * 256:h * 256 + HD] = value[j * cap:(j + 1) * cap, h * HD:(h + 1) * HD]

    def masks():
        whole(cnt.at[pl.ds(1, NSEQ - 1)], csend, crecv).wait_recv()
        tall = cnt[:, 0, :]
        for o in range(2):
            shape = (NSEQ, spans[o])
            r = lax.broadcasted_iota(I32, shape, 0)
            g, hi, dy = r >> 3, (r >> 2) & 1, r & 3
            dz = jnp.where(hi == 0, g, jnp.where(g == 0, 4, NZ - g))
            src = (((s // NY) - dz) & (NZ - 1)) * NY + (((s % NY) - dy) & (NY - 1))
            off = lax.broadcasted_iota(I32, shape, 1) - src * caps[o]
            mine = rank_of(lax.broadcasted_iota(I32, (NSEQ, 128), 1)) == NSEQ * o + s
            have = jnp.sum(jnp.where(mine, tall, 0.0), axis=1, keepdims=True)
            held = jnp.where((off >= 0) & (off.astype(F32) < have), 1.0, 0.0)
            held = jnp.sum(held, axis=0, keepdims=True)
            biases[o][...] = jnp.broadcast_to((1.0 - held) * NEG, (8, spans[o]))

    def columns():
        cl = lax.broadcasted_iota(I32, (BLK, 128), 1)
        lower = (i1 < i0).astype(F32).astype(BF)
        past = first_row(rank_of(lax.broadcasted_iota(I32, (1, 128), 1)), s, caps).astype(F32)
        for b in range(TOK // BLK):
            wide = (cl == col_ref[b * BLK:(b + 1) * BLK]).astype(F32)
            ahead = jnp.dot(lower, wide.astype(BF), preferred_element_type=F32) + past
            dcol[b * BLK:(b + 1) * BLK, :] = jnp.sum(ahead * wide, axis=1, keepdims=True).astype(I32)
            past = past + jnp.sum(wide, axis=0, keepdims=True)

    def attend(o, i):
        lo, hi = i * BLK, (i + 1) * BLK
        dims = (((1,), (1,)), ((), ()))
        below = i0 >= i1

        def head(h, carry):
            lanes = pl.ds(pl.multiple_of(h * HD, HD), HD)
            query = qs[o][lo:hi, lanes]
            bias = biases[o][0:1, :]
            near = lax.dot_general(query, query, dims, preferred_element_type=F32) * FOLD
            near = jnp.where(below, near + bias[:, lo:hi], NEG)
            scores = near
            if i:
                keys = qs[o][0:lo, lanes]
                past = lax.dot_general(query, keys, dims, preferred_element_type=F32) * FOLD
                scores = jnp.concatenate([past + bias[:, :lo], near], axis=1)
            top = jnp.max(scores, axis=1, keepdims=True)
            expo = jnp.exp2(scores - top).astype(BF)
            values = vs[o][0:hi, pl.ds(pl.multiple_of(h * 256, 256), 256)]
            got = jnp.dot(expo, values, preferred_element_type=F32)
            atts[o][lo:hi, lanes] = (got[:, :HD] / got[:, HD:HD + 1]).astype(BF)
            return carry

        lax.fori_loop(0, 2, head, 0)

    def back_copy(o, r):
        src = peer_of(s, r, -1)
        return pltpu.make_async_remote_copy(
            src_ref=atts[o].at[pl.ds(pl.multiple_of(src * caps[o], 16), caps[o])],
            dst_ref=backs[o].at[pl.ds(pl.multiple_of(r * caps[o], 16), caps[o])],
            send_sem=bsend.at[o],
            recv_sem=brecv.at[o],
            device_id=(src, m),
            device_id_type=MESH,
        )

    def give_back(o):
        def send(r, carry):
            back_copy(o, r).start()
            return carry

        lax.fori_loop(1, NSEQ, send, 0)
        backs[o][0:caps[o]] = atts[o][pl.ds(pl.multiple_of(s * caps[o], 16), caps[o])]

    def returned(o):
        ref = backs[o].at[pl.ds(caps[o], (NSEQ - 1) * caps[o])]
        return whole(ref, bsend.at[o], brecv.at[o])

    ring = Ring([(Gs[o], g) for o, g in order], s, m, ssem1, rsem1)
    for t in range(2 * GROUPS + 3):
        ring.step(t, ready, project)
        if t < 2:
            scatter(*order[GROUPS + 2 * t])
            scatter(*order[GROUPS + 2 * t + 1])
        if t == 1:
            lax.fori_loop(1, NSEQ, send_count, 0)
        if t == 6:
            masks()
            attend(0, 0)
            attend(0, 1)
            attend(0, 2)
        if t == 7:
            attend(0, 3)
            attend(0, 4)
        if t == 8:
            attend(0, 5)
            give_back(0)
    for i in range(spans[1] // BLK):
        attend(1, i)
    give_back(1)

    loads[2].wait()

    def wcopy(i, block, to):
        return pltpu.make_async_remote_copy(
            src_ref=wo.at[:, pl.ds(pl.multiple_of(to * 256, 256), 256)],
            dst_ref=wcol.at[block],
            send_sem=wsend.at[i],
            recv_sem=wrecv.at[i],
            device_id=(s, to),
            device_id_type=MESH,
        )

    for i in range(1, NMP):
        wcopy(i, m, lax.rem(m + i, NMP)).start()
    wcol[m] = wo[:, pl.ds(pl.multiple_of(m * 256, 256), 256)]

    columns()
    returned(0).wait_recv()
    returned(1).wait_recv()

    def unpick(k):
        at = dcol[k * BLK:(k + 1) * BLK, :]
        got = jnp.zeros((BLK, 256), F32)
        for o in range(2):
            col = lax.broadcasted_iota(I32, (BLK, spans[o]), 1) + o * spans[0]
            pick = (col == at).astype(F32).astype(BF)
            got = got + jnp.dot(pick, backs[o][...], preferred_element_type=F32)
        G2[m, k] = got.astype(BF)

    def mix(k):
        if k == 0:
            for i in range(1, NMP):
                wcopy(i, lax.rem(m + NMP - i, NMP), lax.rem(m + i, NMP)).wait_recv()
        rows = jnp.concatenate([G2[i, k] for i in range(NMP)], axis=1)
        w = wcol[...].reshape(NMP * 256, 256)
        got = jnp.dot(rows, w, preferred_element_type=F32)
        out_ref[k * BLK:(k + 1) * BLK] = got.astype(BF)

    ring2 = Ring([(G2, k) for k in range(TOK // BLK)], s, m, ssem2, rsem2)
    for t in range(TOK // BLK + 3):
        ring2.step(t, unpick, mix)

    ring.drain()
    ring2.drain()
    for o, g in order:
        landed(o, g, bufs[o].at[g]).wait_send()
    whole(cnt.at[pl.ds(1, NSEQ - 1)], csend, crecv).wait_send()
    for o in range(2):
        returned(o).wait_send()
    for i in range(1, NMP):
        wcopy(i, m, lax.rem(m + i, NMP)).wait_send()


def layer(tokens, cluster_ids, w_query, w_value, w_out, caps, cid):
    vmem = pl.BlockSpec(memory_space=pltpu.VMEM)
    hbm = pl.BlockSpec(memory_space=pl.ANY)
    dma = pltpu.SemaphoreType.DMA
    spans = (NSEQ * caps[0], NSEQ * caps[1])
    chunks = TOK // BLK
    return pl.pallas_call(
        functools.partial(layer_kernel, caps=caps),
        out_shape=jax.ShapeDtypeStruct((TOK, 256), BF),
        in_specs=[vmem, vmem, vmem, hbm, hbm, hbm],
        out_specs=vmem,
        scratch_shapes=[
            pltpu.VMEM((2048, 256), BF),
            pltpu.VMEM((2048, 256), BF),
            pltpu.VMEM((256, 2048), BF),
            pltpu.VMEM((NMP, 256, 256), BF),
            pltpu.VMEM((GROUPS, 8 * caps[0], 256), BF),
            pltpu.VMEM((GROUPS, 8 * caps[1], 256), BF),
            pltpu.VMEM((NMP, GROUPS, 8 * caps[0], 256), BF),
            pltpu.VMEM((NMP, GROUPS, 8 * caps[1], 256), BF),
            pltpu.VMEM((spans[0], 256), BF),
            pltpu.VMEM((spans[1], 256), BF),
            pltpu.VMEM((spans[0], 512), BF),
            pltpu.VMEM((spans[1], 512), BF),
            pltpu.VMEM((8, spans[0]), F32),
            pltpu.VMEM((8, spans[1]), F32),
            pltpu.VMEM((spans[0], 256), BF),
            pltpu.VMEM((spans[1], 256), BF),
            pltpu.VMEM((spans[0], 256), BF),
            pltpu.VMEM((spans[1], 256), BF),
            pltpu.VMEM((NMP, chunks, BLK, 256), BF),
            pltpu.VMEM((NSEQ, 8, 128), F32),
            pltpu.VMEM((128, TOK), BF),
            pltpu.VMEM((1, TOK), I32),
            pltpu.VMEM((TOK, 1), I32),
            dma((3,)),
            dma((8, 2 * GROUPS)), dma((8, 2 * GROUPS)),
            dma((8, chunks)), dma((8, chunks)),
            dma((2 * GROUPS,)), dma((2 * GROUPS,)),
            dma, dma,
            dma((2,)), dma((2,)),
            dma((NMP,)), dma((NMP,)),
        ],
        compiler_params=pltpu.CompilerParams(
            collective_id=cid, has_side_effects=True, vmem_limit_bytes=60 * 1024 * 1024
        ),
        name="layer",
    )(tokens, cluster_ids.reshape(1, TOK), cluster_ids, w_query, w_value, w_out)


def shards(tokens, cluster_ids, w_query, w_value, w_out):
    return layer(tokens, cluster_ids, w_query, w_value, w_out, (CAP, CAP), 1)


def solution(mesh):
    return jax.shard_map(
        shards,
        mesh=mesh,
        in_specs=(P("seq", "mp"), P("seq", None), P(None, "mp"), P(None, "mp"), P("mp", None)),
        out_specs=P("seq", "mp"),
        check_vma=False,
    )
```

```python
import functools

import jax
import jax.numpy as jnp
import numpy as np
from jax import lax
from jax.experimental import pallas as pl
from jax.experimental.pallas import tpu as pltpu
from jax.sharding import PartitionSpec as P

HD = 128
CAP = 48
NZ, NY, NX = 8, 4, 4
NSEQ = NZ * NY
NMP = 2 * NX
TOK = 1536
BLK = 256
NEG = -1e30
MESH = pl.DeviceIdType.MESH
BF = jnp.bfloat16
F32 = jnp.float32
I32 = jnp.int32
FOLD = np.float32(1.4426950408889634 / np.sqrt(128.0))


def peer_of(s, r, sign):
    g, hi, dy = r // 8, (r // 4) % 2, r % 4
    minus = jnp.where(g == 0, 4, NZ - g)
    dz = jnp.where(hi == 0, g, minus)
    z, y = s // NY, s % NY
    return ((z + sign * dz + NZ) % NZ) * NY + (y + sign * dy + NY) % NY


def rank_of(cluster):
    return (cluster & 1) * NSEQ + (cluster >> 1)


def slot_of(s, src):
    dz = (s // NY - src // NY + NZ) % NZ
    hi = dz // 4
    g = (1 - hi) * dz + hi * ((NZ - dz) % 4)
    return g * 8 + hi * 4 + (s % NY - src % NY + NY) % NY


def first_row(rank, s, caps):
    z, y = s // NY, s % NY
    owner, o = rank & (NSEQ - 1), rank >> 5
    dz = ((owner >> 2) - z) & (NZ - 1)
    dy = ((owner & 3) - y) & (NY - 1)
    hi = dz >> 2
    g = jnp.where(hi == 1, (NZ - dz) & 3, dz)
    r = g * 8 + hi * 4 + dy
    return jnp.where(o == 0, r * caps[0], NSEQ * caps[0] + r * caps[1])


class Ring:
    def __init__(self, chunks, s, m, ssem, rsem):
        self.chunks, self.s, self.m = chunks, s, m
        self.ssem, self.rsem = ssem, rsem
        x, c = m // 2, m % 2
        self.right = ((x + 1) % NX) * 2 + c
        self.left = ((x + NX - 1) % NX) * 2 + c
        self.far = ((x + 2) % NX) * 2 + c
        self.sib = x * 2 + 1 - c

    def _copy(self, kind, k, block, to, half=None):
        G, p = self.chunks[k]
        ref = G.at[block, p]
        if half is not None:
            h = G.shape[2] // 2
            ref = G.at[block, p, pl.ds(half * h, h)]
        return pltpu.make_async_remote_copy(
            src_ref=ref,
            dst_ref=ref,
            send_sem=self.ssem.at[kind, k],
            recv_sem=self.rsem.at[kind, k],
            device_id=(self.s, to),
            device_id_type=MESH,
        )

    def send(self, i, k):
        block, to, half = (
            (self.m, self.right, None),
            (self.m, self.left, None),
            (self.m, self.sib, None),
            (self.left, self.right, 0),
            (self.right, self.left, 1),
            (self.left, self.sib, None),
            (self.right, self.sib, None),
            (self.far, self.sib, None),
        )[i]
        return self._copy(i, k, block, to, half)

    def arrival(self, i, k):
        other = lambda block: (block // 2) * 2 + 1 - block % 2
        block, half = (
            (self.left, None),
            (self.right, None),
            (self.sib, None),
            (self.far, 0),
            (self.far, 1),
            (other(self.left), None),
            (other(self.right), None),
            (other(self.far), None),
        )[i]
        return self._copy(i, k, block, self.sib, half)

    def own(self, k):
        for i in (0, 1, 2):
            self.send(i, k).start()

    def near(self, k):
        self.arrival(0, k).wait_recv()
        self.send(3, k).start()
        self.send(5, k).start()
        self.arrival(1, k).wait_recv()
        self.send(4, k).start()
        self.send(6, k).start()

    def across(self, k):
        self.arrival(3, k).wait_recv()
        self.arrival(4, k).wait_recv()
        self.send(7, k).start()

    def shared(self, k):
        for i in (2, 5, 6, 7):
            self.arrival(i, k).wait_recv()

    def drain(self):
        for k in range(len(self.chunks)):
            for i in range(8):
                self.send(i, k).wait_send()


def greet(s, m, mp_peers):
    barrier = pltpu.get_barrier_semaphore()

    def hello(r, carry):
        pl.semaphore_signal(
            barrier, inc=1, device_id=(peer_of(s, r, 1), m), device_id_type=MESH
        )
        return carry

    lax.fori_loop(1, NSEQ, hello, 0)
    for i in range(1, 1 + mp_peers):
        pl.semaphore_signal(
            barrier, inc=1, device_id=(s, lax.rem(m + i, NMP)), device_id_type=MESH
        )
    return barrier


def column(row, n):
    eye = lax.broadcasted_iota(I32, (n, n), 0) == lax.broadcasted_iota(I32, (n, n), 1)
    return jnp.sum(jnp.where(eye, row, 0.0), axis=1, keepdims=True)


def layer_kernel(
    tok_ref, row_ref, wq_hbm, wv_hbm, wo_hbm,
    out_ref,
    wq, wv, wo, wcol, buf0, buf1, G0, G1, q0, q1, v0, v1, have0, have1,
    att0, att1, back0, back1, G2, cnt, onehot, drow, dcol,
    lsem, ssem1, rsem1, ssem2, rsem2, dsend, drecv, csend, crecv,
    bsend, brecv, wsend, wrecv,
    *, caps, parts,
):
    s, m = lax.axis_index("seq"), lax.axis_index("mp")
    bufs, Gs, qs, vs = (buf0, buf1), (G0, G1), (q0, q1), (v0, v1)
    haves, atts, backs = (have0, have1), (att0, att1), (back0, back1)
    spans = (NSEQ * caps[0], NSEQ * caps[1])
    per = [NSEQ // n for n in parts]
    most = max(parts)

    loads = [
        pltpu.make_async_copy(a, b, lsem.at[i])
        for i, (a, b) in enumerate(((wq_hbm, wq), (wv_hbm, wv), (wo_hbm, wo)))
    ]
    for one in loads:
        one.start()

    barrier = greet(s, m, NMP - 1)

    i0 = lax.broadcasted_iota(I32, (BLK, BLK), 0)
    i1 = lax.broadcasted_iota(I32, (BLK, BLK), 1)
    upper = (i0 < i1).astype(F32).astype(BF)
    onehot[...] = (
        lax.broadcasted_iota(I32, (128, TOK), 0) == row_ref[...]
    ).astype(F32).astype(BF)
    rank = rank_of(lax.broadcasted_iota(I32, (1, 128), 1))
    seen = first_row(rank_of(lax.broadcasted_iota(I32, (128, 1), 0)), s, caps).astype(F32)
    for b in range(TOK // BLK):
        part = onehot[:, b * BLK:(b + 1) * BLK]
        wide = part.astype(F32)
        ahead = jnp.dot(part, upper, preferred_element_type=F32) + seen
        drow[:, b * BLK:(b + 1) * BLK] = jnp.sum(ahead * wide, axis=0, keepdims=True).astype(I32)
        seen = seen + jnp.sum(wide, axis=1, keepdims=True)
    pl.semaphore_wait(barrier, NSEQ - 1 + NMP - 1)

    def whole(ref, sem_s, sem_r):
        return pltpu.make_async_remote_copy(
            src_ref=ref, dst_ref=ref, send_sem=sem_s, recv_sem=sem_r,
            device_id=(s, m), device_id_type=MESH,
        )

    def block_copy(o, p, j):
        at = pl.ds(pl.multiple_of(j * caps[o], 16), caps[o])
        return pltpu.make_async_remote_copy(
            src_ref=bufs[o].at[p, at],
            dst_ref=Gs[o].at[m, p, at],
            send_sem=dsend.at[o * most + p],
            recv_sem=drecv.at[o * most + p],
            device_id=(peer_of(s, p * per[o] + j, 1), m),
            device_id_type=MESH,
        )

    def landed(o, p, ref):
        if p == 0:
            ref = ref.at[pl.ds(caps[o], (per[o] - 1) * caps[o])]
        return whole(ref, dsend.at[o * most + p], drecv.at[o * most + p])

    def scatter(o, p):
        n = per[o] * caps[o]
        row = lax.broadcasted_iota(I32, (n, TOK), 0) + (o * spans[0] + p * n)
        pick = (row == drow[...]).astype(F32).astype(BF)
        rows = jnp.dot(pick, tok_ref[...], preferred_element_type=F32).astype(BF)
        bufs[o][p] = rows
        if p == 0:
            Gs[o][m, 0, 0:caps[o]] = rows[0:caps[o]]

        def send(j, carry):
            block_copy(o, p, j).start()
            return carry

        lax.fori_loop(1 if p == 0 else 0, per[o], send, 0)

    turn = {2: (0, 1), 4: (1, 2, 3, 0), 8: (0, 2, 3, 4, 5, 6, 7, 1)}
    order = [(o, p) for o in range(2) for p in turn[parts[o]]]
    scattered = iter(order)

    def scatter_next(count):
        for _, (o, p) in zip(range(count), scattered):
            scatter(o, p)

    scatter_next(3)

    def ready(t):
        o, p = order[t]
        landed(o, p, Gs[o].at[m, p]).wait_recv()

    def project(k):
        o, p = order[k]
        if k == 0:
            loads[0].wait()
            loads[1].wait()
        cap = caps[o]
        rows = jnp.concatenate([Gs[o][i, p] for i in range(NMP)], axis=1)
        query = jnp.dot(rows, wq[...], preferred_element_type=F32).astype(BF)
        value = jnp.dot(rows, wv[...], preferred_element_type=F32).astype(BF)
        for j in range(per[o]):
            at = pl.ds(pl.multiple_of(peer_of(s, p * per[o] + j, -1) * cap, 16), cap)
            qs[o][at] = query[j * cap:(j + 1) * cap]
            for h in range(2):
                vs[o][at, h * 256:h * 256 + HD] = value[j * cap:(j + 1) * cap, h * HD:(h + 1) * HD]

    def tell_counts():
        cnt[0] = lax.dot_general(
            jnp.ones((8, TOK), BF), onehot[...], (((1,), (1,)), ((), ())),
            preferred_element_type=F32,
        )

        def send(r, carry):
            pltpu.make_async_remote_copy(
                src_ref=cnt.at[0], dst_ref=cnt.at[r], send_sem=csend, recv_sem=crecv,
                device_id=(peer_of(s, r, 1), m), device_id_type=MESH,
            ).start()
            return carry

        lax.fori_loop(1, NSEQ, send, 0)

    def counts():
        return whole(cnt.at[pl.ds(1, NSEQ - 1)], csend, crecv)

    def mark(o):
        have = jnp.where(rank == NSEQ * o + s, cnt[:, 0, :], 0.0)
        haves[o][...] = jnp.broadcast_to(jnp.sum(have, axis=1, keepdims=True), (NSEQ, HD))
        place = lax.broadcasted_iota(I32, (caps[o], HD), 0).astype(F32)

        def block(r, carry):
            at = pl.ds(pl.multiple_of(peer_of(s, r, -1) * caps[o], 16), caps[o])
            held = (place < haves[o][pl.ds(r, 1), :]).astype(F32).astype(BF)
            for h in range(2):
                vs[o][at, h * 256 + HD:(h + 1) * 256] = held
            return carry

        lax.fori_loop(0, NSEQ, block, 0)

    def columns():
        for b in range(TOK // BLK):
            at = slice(b * BLK, (b + 1) * BLK)
            dcol[at, :] = column(drow[:, at].astype(F32), BLK).astype(I32)

    def attend(o, i):
        lo, hi = i * BLK, (i + 1) * BLK
        dims = (((1,), (1,)), ((), ()))
        below = i0 >= i1
        for h in range(2):
            lanes = slice(h * HD, (h + 1) * HD)
            wide = slice(h * 256, (h + 1) * 256)
            query = qs[o][lo:hi, lanes]
            near = lax.dot_general(query, query, dims, preferred_element_type=F32) * FOLD
            near = jnp.where(below, near, NEG)
            top = jnp.max(near, axis=1, keepdims=True)
            if i:
                past = lax.dot_general(
                    query, qs[o][0:lo, lanes], dims, preferred_element_type=F32
                ) * FOLD
                top = jnp.maximum(top, jnp.max(past, axis=1, keepdims=True))
                got = jnp.dot(
                    jnp.exp2(past - top).astype(BF), vs[o][0:lo, wide],
                    preferred_element_type=F32,
                )
            expo = jnp.exp2(near - top).astype(BF)
            last = jnp.dot(expo, vs[o][lo:hi, wide], preferred_element_type=F32)
            got = got + last if i else last
            total = jnp.maximum(got[:, HD:], 0.5)
            atts[o][lo:hi, lanes] = (got[:, :HD] / total).astype(BF)

    def give_back(o, first, last):
        def send(at, carry):
            src = first + (at - first + s) % (last - first)
            r = slot_of(s, src)
            rows = pl.ds(pl.multiple_of(src * caps[o], 16), caps[o])

            @pl.when(src != s)
            def _():
                pltpu.make_async_remote_copy(
                    src_ref=atts[o].at[rows],
                    dst_ref=backs[o].at[pl.ds(pl.multiple_of(r * caps[o], 16), caps[o])],
                    send_sem=bsend.at[o],
                    recv_sem=brecv.at[o],
                    device_id=(src, m),
                    device_id_type=MESH,
                ).start()

            return carry

        lax.fori_loop(first, last, send, 0)

    def keep(o):
        backs[o][0:caps[o]] = atts[o][pl.ds(pl.multiple_of(s * caps[o], 16), caps[o])]

    def returned(o):
        ref = backs[o].at[pl.ds(caps[o], (NSEQ - 1) * caps[o])]
        return whole(ref, bsend.at[o], brecv.at[o])

    def pairs(o):
        half = spans[o] // BLK // 2
        ends = [(i + 1) * BLK // caps[o] for i in range(2 * half)]
        for i in range(half):
            yield i, ((ends[i - 1] if i else 0, ends[i]), (ends[i + half - 1], ends[i + half]))

    def attend_pair(o, i):
        half = spans[o] // BLK // 2
        for at, (first, last) in zip((i, i + half), dict(pairs(o))[i]):
            attend(o, at)
        for first, last in dict(pairs(o))[i]:
            give_back(o, first, last)
        if i == half - 1:
            keep(o)

    ring = Ring([(Gs[o], p) for o, p in order], s, m, ssem1, rsem1)

    def open_(k):
        ready(k)
        ring.own(k)

    def close(k):
        ring.shared(k)
        project(k)

    first, n = parts[0], len(order)
    half = spans[0] // BLK // 2
    for t in range(n + 3):
        if t < n:
            open_(t)
        scatter_next(2)
        if t == 2:
            tell_counts()
        if 3 <= t:
            close(t - 3)
        if 2 <= t < n + 2:
            ring.across(t - 2)
        if 1 <= t < n + 1:
            ring.near(t - 1)
        if t == first + 2:
            counts().wait_recv()
            mark(0)
        if first + 2 <= t < first + 2 + half:
            attend_pair(0, t - first - 2)
        if t == n:
            mark(1)
    for i in range(spans[1] // BLK // 2):
        attend_pair(1, i)

    loads[2].wait()

    def wcopy(i, block, to):
        return pltpu.make_async_remote_copy(
            src_ref=wo.at[:, pl.ds(pl.multiple_of(to * 256, 256), 256)],
            dst_ref=wcol.at[block],
            send_sem=wsend.at[i],
            recv_sem=wrecv.at[i],
            device_id=(s, to),
            device_id_type=MESH,
        )

    for i in range(1, NMP):
        wcopy(i, m, lax.rem(m + i, NMP)).start()
    wcol[m] = wo[:, pl.ds(pl.multiple_of(m * 256, 256), 256)]

    columns()
    returned(0).wait_recv()
    returned(1).wait_recv()

    def unpick(k):
        at = dcol[k * BLK:(k + 1) * BLK, :]
        got = jnp.zeros((BLK, 256), F32)
        for o in range(2):
            col = lax.broadcasted_iota(I32, (BLK, spans[o]), 1) + o * spans[0]
            pick = (col == at).astype(F32).astype(BF)
            got = got + jnp.dot(pick, backs[o][...], preferred_element_type=F32)
        G2[m, k] = got.astype(BF)

    def mix(k):
        if k == 0:
            for i in range(1, NMP):
                wcopy(i, lax.rem(m + NMP - i, NMP), lax.rem(m + i, NMP)).wait_recv()
        rows = jnp.concatenate([G2[i, k] for i in range(NMP)], axis=1)
        w = wcol[...].reshape(NMP * 256, 256)
        got = jnp.dot(rows, w, preferred_element_type=F32)
        out_ref[k * BLK:(k + 1) * BLK] = got.astype(BF)

    ring2 = Ring([(G2, k) for k in range(TOK // BLK)], s, m, ssem2, rsem2)
    n = TOK // BLK
    for t in range(n + 3):
        if t < n:
            unpick(t)
            ring2.own(t)
        if 3 <= t:
            ring2.shared(t - 3)
            mix(t - 3)
        if 2 <= t < n + 2:
            ring2.across(t - 2)
        if 1 <= t < n + 1:
            ring2.near(t - 1)

    ring.drain()
    ring2.drain()
    for o, p in order:
        landed(o, p, bufs[o].at[p]).wait_send()
    counts().wait_send()
    for o in range(2):
        returned(o).wait_send()
    for i in range(1, NMP):
        wcopy(i, m, lax.rem(m + i, NMP)).wait_send()


def layer(tokens, ids, w_query, w_value, w_out, caps, parts, cid):
    vmem = pl.BlockSpec(memory_space=pltpu.VMEM)
    hbm = pl.BlockSpec(memory_space=pl.ANY)
    dma = pltpu.SemaphoreType.DMA
    spans = (NSEQ * caps[0], NSEQ * caps[1])
    chunks, most = TOK // BLK, max(parts)
    buf = [pltpu.VMEM((n, span // n, 256), BF) for n, span in zip(parts, spans)]
    G = [pltpu.VMEM((NMP, n, span // n, 256), BF) for n, span in zip(parts, spans)]
    flat = [pltpu.VMEM((span, 256), BF) for span in spans]
    return pl.pallas_call(
        functools.partial(layer_kernel, caps=caps, parts=parts),
        out_shape=jax.ShapeDtypeStruct((TOK, 256), BF),
        in_specs=[vmem] * 2 + [hbm] * 3,
        out_specs=vmem,
        scratch_shapes=[
            pltpu.VMEM((2048, 256), BF),
            pltpu.VMEM((2048, 256), BF),
            pltpu.VMEM((256, 2048), BF),
            pltpu.VMEM((NMP, 256, 256), BF),
            *buf,
            *G,
            *flat,
            *[pltpu.VMEM((span, 512), BF) for span in spans],
            *[pltpu.VMEM((NSEQ, HD), F32)] * 2,
            *flat,
            *flat,
            pltpu.VMEM((NMP, chunks, BLK, 256), BF),
            pltpu.VMEM((NSEQ, 8, 128), F32),
            pltpu.VMEM((128, TOK), BF),
            pltpu.VMEM((1, TOK), I32),
            pltpu.VMEM((TOK, 1), I32),
            dma((3,)),
            dma((8, sum(parts))), dma((8, sum(parts))),
            dma((8, chunks)), dma((8, chunks)),
            dma((2 * most,)), dma((2 * most,)),
            dma, dma,
            dma((2,)), dma((2,)),
            dma((NMP,)), dma((NMP,)),
        ],
        compiler_params=pltpu.CompilerParams(
            collective_id=cid, has_side_effects=True, vmem_limit_bytes=60 * 1024 * 1024
        ),
        name="layer",
    )(tokens, ids, w_query, w_value, w_out)


def shards(tokens, cluster_ids, w_query, w_value, w_out):
    ids = cluster_ids.reshape(1, TOK)
    return layer(tokens, ids, w_query, w_value, w_out, (CAP, CAP), (4, 4), 1)


def solution(mesh):
    return jax.shard_map(
        shards,
        mesh=mesh,
        in_specs=(P("seq", "mp"), P("seq", None), P(None, "mp"), P(None, "mp"), P("mp", None)),
        out_specs=P("seq", "mp"),
        check_vma=False,
    )
```

```python
import functools

import jax
import jax.numpy as jnp
import numpy as np
from jax import lax
from jax.experimental import pallas as pl
from jax.experimental.pallas import tpu as pltpu
from jax.sharding import PartitionSpec as P

HD = 128
CAP = 48
NZ, NY, NX = 8, 4, 4
NSEQ = NZ * NY
NMP = 2 * NX
TOK = 1536
BLK = 256
ROWS = 256
AHEAD = 1
FIRST = ((0, 4), (8, 8), (16, 8), (24, 8), (4, 4))
SECOND = ((8, 8), (16, 8), (24, 8), (0, 8))
NEG = -1e30
MESH = pl.DeviceIdType.MESH
BF = jnp.bfloat16
F32 = jnp.float32
I32 = jnp.int32
FOLD = np.float32(1.4426950408889634 / np.sqrt(128.0))


def peer_of(s, r, sign):
    g, hi, dy = r // 8, (r // 4) % 2, r % 4
    minus = jnp.where(g == 0, 4, NZ - g)
    dz = jnp.where(hi == 0, g, minus)
    z, y = s // NY, s % NY
    return ((z + sign * dz + NZ) % NZ) * NY + (y + sign * dy + NY) % NY


def rank_of(cluster):
    return (cluster & 1) * NSEQ + (cluster >> 1)


def slot_of(s, src):
    dz = (s // NY - src // NY + NZ) % NZ
    hi = dz // 4
    g = (1 - hi) * dz + hi * ((NZ - dz) % 4)
    return g * 8 + hi * 4 + (s % NY - src % NY + NY) % NY


def first_row(rank, s, caps):
    z, y = s // NY, s % NY
    owner, o = rank & (NSEQ - 1), rank >> 5
    dz = ((owner >> 2) - z) & (NZ - 1)
    dy = ((owner & 3) - y) & (NY - 1)
    hi = dz >> 2
    g = jnp.where(hi == 1, (NZ - dz) & 3, dz)
    r = g * 8 + hi * 4 + dy
    return jnp.where(o == 0, r * caps[0], NSEQ * caps[0] + r * caps[1])


class Ring:
    def __init__(self, chunks, s, m, ssem, rsem):
        self.chunks, self.s, self.m = chunks, s, m
        self.ssem, self.rsem = ssem, rsem
        x, c = m // 2, m % 2
        self.right = ((x + 1) % NX) * 2 + c
        self.left = ((x + NX - 1) % NX) * 2 + c
        self.far = ((x + 2) % NX) * 2 + c
        self.sib = x * 2 + 1 - c

    def _copy(self, kind, k, block, to, half=None):
        G, start, rows = self.chunks[k]
        if half is not None:
            rows = rows // 2
            start = start + half * rows
        ref = G.at[block, pl.ds(start, rows)]
        return pltpu.make_async_remote_copy(
            src_ref=ref,
            dst_ref=ref,
            send_sem=self.ssem.at[kind, k],
            recv_sem=self.rsem.at[kind, k],
            device_id=(self.s, to),
            device_id_type=MESH,
        )

    def send(self, i, k):
        block, to, half = (
            (self.m, self.right, None),
            (self.m, self.left, None),
            (self.m, self.sib, None),
            (self.left, self.right, 0),
            (self.right, self.left, 1),
            (self.left, self.sib, None),
            (self.right, self.sib, None),
            (self.far, self.sib, None),
        )[i]
        return self._copy(i, k, block, to, half)

    def arrival(self, i, k):
        other = lambda block: (block // 2) * 2 + 1 - block % 2
        block, half = (
            (self.left, None),
            (self.right, None),
            (self.sib, None),
            (self.far, 0),
            (self.far, 1),
            (other(self.left), None),
            (other(self.right), None),
            (other(self.far), None),
        )[i]
        return self._copy(i, k, block, self.sib, half)

    def own(self, k):
        for i in (0, 1, 2):
            self.send(i, k).start()

    def near(self, k):
        self.arrival(0, k).wait_recv()
        self.send(3, k).start()
        self.send(5, k).start()
        self.arrival(1, k).wait_recv()
        self.send(4, k).start()
        self.send(6, k).start()

    def across(self, k):
        self.arrival(3, k).wait_recv()
        self.arrival(4, k).wait_recv()
        self.send(7, k).start()

    def shared(self, k):
        for i in (2, 5, 6, 7):
            self.arrival(i, k).wait_recv()

    def drain(self):
        for k in range(len(self.chunks)):
            for i in range(8):
                self.send(i, k).wait_send()


def greet(s, m, mp_peers):
    barrier = pltpu.get_barrier_semaphore()

    def hello(r, carry):
        pl.semaphore_signal(
            barrier, inc=1, device_id=(peer_of(s, r, 1), m), device_id_type=MESH
        )
        return carry

    lax.fori_loop(1, NSEQ, hello, 0)
    for i in range(1, 1 + mp_peers):
        pl.semaphore_signal(
            barrier, inc=1, device_id=(s, lax.rem(m + i, NMP)), device_id_type=MESH
        )
    return barrier


def column(row, n):
    eye = lax.broadcasted_iota(I32, (n, n), 0) == lax.broadcasted_iota(I32, (n, n), 1)
    return jnp.sum(jnp.where(eye, row, 0.0), axis=1, keepdims=True)


def layer_kernel(
    row_ref, tok_hbm, wq_hbm, wv_hbm, wo_hbm,
    out_ref,
    tok_ref, wq, wv, wo, wcol, buf0, buf1, G0, G1, q0, q1, v0, v1, have0, have1,
    att0, att1, back0, back1, G2, cnt, onehot, drow, dcol,
    lsem, ssem1, rsem1, ssem2, rsem2, dsend, drecv, csend, crecv,
    bsend, brecv, wsend, wrecv,
    *, caps, parts,
):
    s, m = lax.axis_index("seq"), lax.axis_index("mp")
    bufs, Gs, qs, vs = (buf0, buf1), (G0, G1), (q0, q1), (v0, v1)
    haves, atts, backs = (have0, have1), (att0, att1), (back0, back1)
    spans = (NSEQ * caps[0], NSEQ * caps[1])

    loads = [
        pltpu.make_async_copy(a, b, lsem.at[i])
        for i, (a, b) in enumerate(
            ((wq_hbm, wq), (wv_hbm, wv), (wo_hbm, wo), (tok_hbm, tok_ref))
        )
    ]
    barrier = greet(s, m, NMP - 1)
    for i in (3, 0, 1, 2):
        loads[i].start()

    i0 = lax.broadcasted_iota(I32, (BLK, BLK), 0)
    i1 = lax.broadcasted_iota(I32, (BLK, BLK), 1)
    upper = (i0 < i1).astype(F32).astype(BF)
    onehot[...] = (
        lax.broadcasted_iota(I32, (128, TOK), 0) == row_ref[...]
    ).astype(F32).astype(BF)
    rank = rank_of(lax.broadcasted_iota(I32, (1, 128), 1))
    seen = first_row(rank_of(lax.broadcasted_iota(I32, (128, 1), 0)), s, caps).astype(F32)
    for b in range(TOK // BLK):
        part = onehot[:, b * BLK:(b + 1) * BLK]
        wide = part.astype(F32)
        ahead = jnp.dot(part, upper, preferred_element_type=F32) + seen
        drow[:, b * BLK:(b + 1) * BLK] = jnp.sum(ahead * wide, axis=0, keepdims=True).astype(I32)
        seen = seen + jnp.sum(wide, axis=1, keepdims=True)
    pl.semaphore_wait(barrier, NSEQ - 1 + NMP - 1)

    def whole(ref, sem_s, sem_r):
        return pltpu.make_async_remote_copy(
            src_ref=ref, dst_ref=ref, send_sem=sem_s, recv_sem=sem_r,
            device_id=(s, m), device_id_type=MESH,
        )

    def block_copy(k, r):
        o = order[k][0]
        at = pl.ds(pl.multiple_of(r * caps[o], 16), caps[o])
        return pltpu.make_async_remote_copy(
            src_ref=bufs[o].at[at],
            dst_ref=Gs[o].at[m, at],
            send_sem=dsend.at[k],
            recv_sem=drecv.at[k],
            device_id=(peer_of(s, r, 1), m),
            device_id_type=MESH,
        )

    def rows_of(k):
        o, r, n = order[k]
        return r * caps[o], n * caps[o]

    def landed(k, ref):
        start, rows = rows_of(k)
        if start == 0:
            start, rows = caps[order[k][0]], rows - caps[order[k][0]]
        return whole(ref.at[pl.ds(start, rows)], dsend.at[k], drecv.at[k])

    def scatter(k):
        o, r, n = order[k]
        start, rows = rows_of(k)
        row = lax.broadcasted_iota(I32, (rows, TOK), 0) + (o * spans[0] + start)
        pick = (row == drow[...]).astype(F32).astype(BF)
        got = jnp.dot(pick, tok_ref[...], preferred_element_type=F32).astype(BF)
        bufs[o][start:start + rows] = got
        if r == 0:
            Gs[o][m, 0:caps[o]] = got[0:caps[o]]

        def send(at, carry):
            block_copy(k, at).start()
            return carry

        lax.fori_loop(max(r, 1), r + n, send, 0)

    order = [(o, r, n) for o in range(2) for r, n in parts[o]]
    scattered = iter(range(len(order)))

    def scatter_next(count):
        for _, k in zip(range(count), scattered):
            scatter(k)

    loads[3].wait()
    scatter_next(3)

    def ready(t):
        landed(t, Gs[order[t][0]].at[m]).wait_recv()

    def project(k):
        o, r, n = order[k]
        start, size = rows_of(k)
        if k == 0:
            loads[0].wait()
            loads[1].wait()
        cap = caps[o]
        rows = jnp.concatenate([Gs[o][i, start:start + size] for i in range(NMP)], axis=1)
        query = jnp.dot(rows, wq[...], preferred_element_type=F32).astype(BF)
        value = jnp.dot(rows, wv[...], preferred_element_type=F32).astype(BF)
        for j in range(n):
            at = pl.ds(pl.multiple_of(peer_of(s, r + j, -1) * cap, 16), cap)
            qs[o][at] = query[j * cap:(j + 1) * cap]
            for h in range(2):
                vs[o][at, h * 256:h * 256 + HD] = value[j * cap:(j + 1) * cap, h * HD:(h + 1) * HD]

    def tell_counts():
        cnt[0] = lax.dot_general(
            jnp.ones((8, TOK), BF), onehot[...], (((1,), (1,)), ((), ())),
            preferred_element_type=F32,
        )

        def send(r, carry):
            pltpu.make_async_remote_copy(
                src_ref=cnt.at[0], dst_ref=cnt.at[r], send_sem=csend, recv_sem=crecv,
                device_id=(peer_of(s, r, 1), m), device_id_type=MESH,
            ).start()
            return carry

        lax.fori_loop(1, NSEQ, send, 0)

    def counts():
        return whole(cnt.at[pl.ds(1, NSEQ - 1)], csend, crecv)

    def mark(o):
        have = jnp.where(rank == NSEQ * o + s, cnt[:, 0, :], 0.0)
        haves[o][...] = jnp.broadcast_to(jnp.sum(have, axis=1, keepdims=True), (NSEQ, HD))
        place = lax.broadcasted_iota(I32, (caps[o], HD), 0).astype(F32)

        def block(r, carry):
            at = pl.ds(pl.multiple_of(peer_of(s, r, -1) * caps[o], 16), caps[o])
            held = (place < haves[o][pl.ds(r, 1), :]).astype(F32).astype(BF)
            for h in range(2):
                vs[o][at, h * 256 + HD:(h + 1) * 256] = held
            return carry

        lax.fori_loop(0, NSEQ, block, 0)

    def columns():
        for b in range(TOK // BLK):
            at = slice(b * BLK, (b + 1) * BLK)
            dcol[at, :] = column(drow[:, at].astype(F32), BLK).astype(I32)

    def attend(o, i):
        lo, hi = i * BLK, (i + 1) * BLK
        dims = (((1,), (1,)), ((), ()))
        below = i0 >= i1
        for h in range(2):
            lanes = slice(h * HD, (h + 1) * HD)
            wide = slice(h * 256, (h + 1) * 256)
            query = qs[o][lo:hi, lanes]
            near = lax.dot_general(query, query, dims, preferred_element_type=F32) * FOLD
            near = jnp.where(below, near, NEG)
            top = jnp.max(near, axis=1, keepdims=True)
            if i:
                past = lax.dot_general(
                    query, qs[o][0:lo, lanes], dims, preferred_element_type=F32
                ) * FOLD
                top = jnp.maximum(top, jnp.max(past, axis=1, keepdims=True))
                got = jnp.dot(
                    jnp.exp2(past - top).astype(BF), vs[o][0:lo, wide],
                    preferred_element_type=F32,
                )
            expo = jnp.exp2(near - top).astype(BF)
            last = jnp.dot(expo, vs[o][lo:hi, wide], preferred_element_type=F32)
            got = got + last if i else last
            total = jnp.maximum(got[:, HD:], 0.5)
            atts[o][lo:hi, lanes] = (got[:, :HD] / total).astype(BF)

    def give_back(o, first, last):
        def send(at, carry):
            src = first + (at - first + s) % (last - first)
            r = slot_of(s, src)
            rows = pl.ds(pl.multiple_of(src * caps[o], 16), caps[o])

            @pl.when(src != s)
            def _():
                pltpu.make_async_remote_copy(
                    src_ref=atts[o].at[rows],
                    dst_ref=backs[o].at[pl.ds(pl.multiple_of(r * caps[o], 16), caps[o])],
                    send_sem=bsend.at[o],
                    recv_sem=brecv.at[o],
                    device_id=(src, m),
                    device_id_type=MESH,
                ).start()

            return carry

        lax.fori_loop(first, last, send, 0)

    def keep(o):
        backs[o][0:caps[o]] = atts[o][pl.ds(pl.multiple_of(s * caps[o], 16), caps[o])]

    def returned(o):
        ref = backs[o].at[pl.ds(caps[o], (NSEQ - 1) * caps[o])]
        return whole(ref, bsend.at[o], brecv.at[o])

    def pairs(o):
        half = spans[o] // BLK // 2
        ends = [(i + 1) * BLK // caps[o] for i in range(2 * half)]
        for i in range(half):
            yield i, ((ends[i - 1] if i else 0, ends[i]), (ends[i + half - 1], ends[i + half]))

    def attend_pair(o, i):
        half = spans[o] // BLK // 2
        for at, (first, last) in zip((i, i + half), dict(pairs(o))[i]):
            attend(o, at)
        for first, last in dict(pairs(o))[i]:
            give_back(o, first, last)
        if i == half - 1:
            keep(o)

    ring = Ring([(Gs[order[k][0]], *rows_of(k)) for k in range(len(order))], s, m, ssem1, rsem1)

    def open_(k):
        ready(k)
        ring.own(k)

    def close(k):
        ring.shared(k)
        project(k)

    first, n = len(parts[0]), len(order)
    half = spans[0] // BLK // 2
    for t in range(n + 3):
        if t < n:
            open_(t)
        scatter_next(2)
        if t == 2:
            tell_counts()
        if 3 <= t:
            close(t - 3)
        if 2 <= t < n + 2:
            ring.across(t - 2)
        if 1 <= t < n + 1:
            ring.near(t - 1)
        if t == first + 2:
            counts().wait_recv()
            mark(0)
        if first + 2 <= t < first + 2 + half:
            attend_pair(0, t - first - 2)
        if t == n:
            mark(1)
    for i in range(spans[1] // BLK // 2):
        attend_pair(1, i)

    loads[2].wait()

    def wcopy(i, block, to):
        return pltpu.make_async_remote_copy(
            src_ref=wo.at[:, pl.ds(pl.multiple_of(to * 256, 256), 256)],
            dst_ref=wcol.at[block],
            send_sem=wsend.at[i],
            recv_sem=wrecv.at[i],
            device_id=(s, to),
            device_id_type=MESH,
        )

    for i in range(1, NMP):
        wcopy(i, m, lax.rem(m + i, NMP)).start()
    wcol[m] = wo[:, pl.ds(pl.multiple_of(m * 256, 256), 256)]

    def unpick(k, o):
        at = dcol[k * ROWS:(k + 1) * ROWS, :]
        col = lax.broadcasted_iota(I32, (ROWS, spans[o]), 1) + o * spans[0]
        pick = (col == at).astype(F32).astype(BF)
        got = jnp.dot(pick, backs[o][...], preferred_element_type=F32).astype(BF)
        at = slice(k * ROWS, (k + 1) * ROWS)
        G2[m, at] = got if o == 0 else got + G2[m, at]

    n = TOK // ROWS
    columns()
    returned(0).wait_recv()
    for k in range(n):
        unpick(k, 0)
    returned(1).wait_recv()

    def mix(k):
        if k == 0:
            for i in range(1, NMP):
                wcopy(i, lax.rem(m + NMP - i, NMP), lax.rem(m + i, NMP)).wait_recv()
        rows = jnp.concatenate(
            [G2[i, k * ROWS:(k + 1) * ROWS] for i in range(NMP)], axis=1
        )
        w = wcol[...].reshape(NMP * 256, 256)
        got = jnp.dot(rows, w, preferred_element_type=F32)
        out_ref[k * ROWS:(k + 1) * ROWS] = got.astype(BF)

    ring2 = Ring([(G2, k * ROWS, ROWS) for k in range(n)], s, m, ssem2, rsem2)
    def send_own(k):
        if k < n:
            unpick(k, 1)
            ring2.own(k)

    for k in range(AHEAD):
        send_own(k)
    for t in range(1, n + 3):
        send_own(t + AHEAD - 1)
        if 3 <= t:
            ring2.shared(t - 3)
            mix(t - 3)
        if 2 <= t < n + 2:
            ring2.across(t - 2)
        if 1 <= t < n + 1:
            ring2.near(t - 1)

    ring.drain()
    ring2.drain()
    for k in range(len(order)):
        landed(k, bufs[order[k][0]]).wait_send()
    counts().wait_send()
    for o in range(2):
        returned(o).wait_send()
    for i in range(1, NMP):
        wcopy(i, m, lax.rem(m + i, NMP)).wait_send()


def layer(tokens, ids, w_query, w_value, w_out, caps, parts, cid):
    vmem = pl.BlockSpec(memory_space=pltpu.VMEM)
    hbm = pl.BlockSpec(memory_space=pl.ANY)
    dma = pltpu.SemaphoreType.DMA
    spans = (NSEQ * caps[0], NSEQ * caps[1])
    chunks, total = TOK // ROWS, sum(len(one) for one in parts)
    G = [pltpu.VMEM((NMP, span, 256), BF) for span in spans]
    flat = [pltpu.VMEM((span, 256), BF) for span in spans]
    return pl.pallas_call(
        functools.partial(layer_kernel, caps=caps, parts=parts),
        out_shape=jax.ShapeDtypeStruct((TOK, 256), BF),
        in_specs=[vmem] + [hbm] * 4,
        out_specs=vmem,
        scratch_shapes=[
            pltpu.VMEM((TOK, 256), BF),
            pltpu.VMEM((2048, 256), BF),
            pltpu.VMEM((2048, 256), BF),
            pltpu.VMEM((256, 2048), BF),
            pltpu.VMEM((NMP, 256, 256), BF),
            *flat,
            *G,
            *flat,
            *[pltpu.VMEM((span, 512), BF) for span in spans],
            *[pltpu.VMEM((NSEQ, HD), F32)] * 2,
            *flat,
            *flat,
            pltpu.VMEM((NMP, TOK, 256), BF),
            pltpu.VMEM((NSEQ, 8, 128), F32),
            pltpu.VMEM((128, TOK), BF),
            pltpu.VMEM((1, TOK), I32),
            pltpu.VMEM((TOK, 1), I32),
            dma((4,)),
            dma((8, total)), dma((8, total)),
            dma((8, chunks)), dma((8, chunks)),
            dma((total,)), dma((total,)),
            dma, dma,
            dma((2,)), dma((2,)),
            dma((NMP,)), dma((NMP,)),
        ],
        compiler_params=pltpu.CompilerParams(
            collective_id=cid, has_side_effects=True, vmem_limit_bytes=60 * 1024 * 1024
        ),
        name="layer",
    )(ids, tokens, w_query, w_value, w_out)


def shards(tokens, cluster_ids, w_query, w_value, w_out):
    ids = cluster_ids.reshape(1, TOK)
    return layer(tokens, ids, w_query, w_value, w_out, (CAP, CAP), (FIRST, SECOND), 1)


def solution(mesh):
    return jax.shard_map(
        shards,
        mesh=mesh,
        in_specs=(P("seq", "mp"), P("seq", None), P(None, "mp"), P(None, "mp"), P("mp", None)),
        out_specs=P("seq", "mp"),
        check_vma=False,
    )
```

```python
import functools

import jax
import jax.numpy as jnp
import numpy as np
from jax import lax
from jax.experimental import pallas as pl
from jax.experimental.pallas import tpu as pltpu
from jax.sharding import PartitionSpec as P

HD = 128
CAP = 48
NZ, NY, NX = 8, 4, 4
NSEQ = NZ * NY
NMP = 2 * NX
TOK = 1536
BLK = 256
ROWS = 384
AHEAD = 1
FIRST = ((0, 4), (8, 8), (16, 8), (24, 8), (4, 4))
SECOND = ((8, 8), (16, 8), (24, 8), (0, 8))
NEG = -1e30
MESH = pl.DeviceIdType.MESH
BF = jnp.bfloat16
F32 = jnp.float32
I32 = jnp.int32
FOLD = np.float32(1.4426950408889634 / np.sqrt(128.0))


def peer_of(s, r, sign):
    g, hi, dy = r // 8, (r // 4) % 2, r % 4
    minus = jnp.where(g == 0, 4, NZ - g)
    dz = jnp.where(hi == 0, g, minus)
    z, y = s // NY, s % NY
    return ((z + sign * dz + NZ) % NZ) * NY + (y + sign * dy + NY) % NY


def rank_of(cluster):
    return (cluster & 1) * NSEQ + (cluster >> 1)


def slot_of(s, src):
    dz = (s // NY - src // NY + NZ) % NZ
    hi = dz // 4
    g = (1 - hi) * dz + hi * ((NZ - dz) % 4)
    return g * 8 + hi * 4 + (s % NY - src % NY + NY) % NY


def first_row(rank, s, caps):
    z, y = s // NY, s % NY
    owner, o = rank & (NSEQ - 1), rank >> 5
    dz = ((owner >> 2) - z) & (NZ - 1)
    dy = ((owner & 3) - y) & (NY - 1)
    hi = dz >> 2
    g = jnp.where(hi == 1, (NZ - dz) & 3, dz)
    r = g * 8 + hi * 4 + dy
    return jnp.where(o == 0, r * caps[0], NSEQ * caps[0] + r * caps[1])


class Ring:
    def __init__(self, chunks, s, m, ssem, rsem):
        self.chunks, self.s, self.m = chunks, s, m
        self.ssem, self.rsem = ssem, rsem
        x, c = m // 2, m % 2
        self.right = ((x + 1) % NX) * 2 + c
        self.left = ((x + NX - 1) % NX) * 2 + c
        self.far = ((x + 2) % NX) * 2 + c
        self.sib = x * 2 + 1 - c

    def _copy(self, kind, k, block, to, half=None):
        G, start, rows = self.chunks[k]
        if half is not None:
            rows = rows // 2
            start = start + half * rows
        ref = G.at[block, pl.ds(start, rows)]
        return pltpu.make_async_remote_copy(
            src_ref=ref,
            dst_ref=ref,
            send_sem=self.ssem.at[kind, k],
            recv_sem=self.rsem.at[kind, k],
            device_id=(self.s, to),
            device_id_type=MESH,
        )

    def send(self, i, k):
        block, to, half = (
            (self.m, self.right, None),
            (self.m, self.left, None),
            (self.m, self.sib, None),
            (self.left, self.right, 0),
            (self.right, self.left, 1),
            (self.left, self.sib, None),
            (self.right, self.sib, None),
            (self.far, self.sib, None),
        )[i]
        return self._copy(i, k, block, to, half)

    def arrival(self, i, k):
        other = lambda block: (block // 2) * 2 + 1 - block % 2
        block, half = (
            (self.left, None),
            (self.right, None),
            (self.sib, None),
            (self.far, 0),
            (self.far, 1),
            (other(self.left), None),
            (other(self.right), None),
            (other(self.far), None),
        )[i]
        return self._copy(i, k, block, self.sib, half)

    def own(self, k):
        for i in (0, 1, 2):
            self.send(i, k).start()

    def near(self, k):
        self.arrival(0, k).wait_recv()
        self.send(3, k).start()
        self.send(5, k).start()
        self.arrival(1, k).wait_recv()
        self.send(4, k).start()
        self.send(6, k).start()

    def across(self, k):
        self.arrival(3, k).wait_recv()
        self.arrival(4, k).wait_recv()
        self.send(7, k).start()

    def shared(self, k):
        for i in (2, 5, 6, 7):
            self.arrival(i, k).wait_recv()

    def drain(self):
        for k in range(len(self.chunks)):
            for i in range(8):
                self.send(i, k).wait_send()


def greet(s, m, mp_peers):
    barrier = pltpu.get_barrier_semaphore()

    def hello(r, carry):
        pl.semaphore_signal(
            barrier, inc=1, device_id=(peer_of(s, r, 1), m), device_id_type=MESH
        )
        return carry

    lax.fori_loop(1, NSEQ, hello, 0)
    for i in range(1, 1 + mp_peers):
        pl.semaphore_signal(
            barrier, inc=1, device_id=(s, lax.rem(m + i, NMP)), device_id_type=MESH
        )
    return barrier


def column(row, n):
    eye = lax.broadcasted_iota(I32, (n, n), 0) == lax.broadcasted_iota(I32, (n, n), 1)
    return jnp.sum(jnp.where(eye, row, 0.0), axis=1, keepdims=True)


def layer_kernel(
    row_ref, tok_hbm, wq_hbm, wv_hbm, wo_hbm,
    out_ref,
    tok_ref, wq, wv, wo, wcol, buf0, buf1, G0, G1, q0, q1, v0, v1, have0, have1,
    att0, att1, back0, back1, G2, cnt, onehot, drow, dcol,
    lsem, ssem1, rsem1, ssem2, rsem2, dsend, drecv, csend, crecv,
    bsend, brecv, wsend, wrecv,
    *, caps, parts,
):
    s, m = lax.axis_index("seq"), lax.axis_index("mp")
    bufs, Gs, qs, vs = (buf0, buf1), (G0, G1), (q0, q1), (v0, v1)
    haves, atts, backs = (have0, have1), (att0, att1), (back0, back1)
    spans = (NSEQ * caps[0], NSEQ * caps[1])

    loads = [
        pltpu.make_async_copy(a, b, lsem.at[i])
        for i, (a, b) in enumerate(
            ((wq_hbm, wq), (wv_hbm, wv), (wo_hbm, wo), (tok_hbm, tok_ref))
        )
    ]
    barrier = greet(s, m, NMP - 1)
    for i in (3, 0, 1, 2):
        loads[i].start()

    i0 = lax.broadcasted_iota(I32, (BLK, BLK), 0)
    i1 = lax.broadcasted_iota(I32, (BLK, BLK), 1)
    upper = (i0 < i1).astype(F32).astype(BF)
    onehot[...] = (
        lax.broadcasted_iota(I32, (128, TOK), 0) == row_ref[...]
    ).astype(F32).astype(BF)
    rank = rank_of(lax.broadcasted_iota(I32, (1, 128), 1))
    seen = first_row(rank_of(lax.broadcasted_iota(I32, (128, 1), 0)), s, caps).astype(F32)
    for b in range(TOK // BLK):
        part = onehot[:, b * BLK:(b + 1) * BLK]
        wide = part.astype(F32)
        ahead = jnp.dot(part, upper, preferred_element_type=F32) + seen
        drow[:, b * BLK:(b + 1) * BLK] = jnp.sum(ahead * wide, axis=0, keepdims=True).astype(I32)
        seen = seen + jnp.sum(wide, axis=1, keepdims=True)
    pl.semaphore_wait(barrier, NSEQ - 1 + NMP - 1)

    def whole(ref, sem_s, sem_r):
        return pltpu.make_async_remote_copy(
            src_ref=ref, dst_ref=ref, send_sem=sem_s, recv_sem=sem_r,
            device_id=(s, m), device_id_type=MESH,
        )

    def block_copy(k, r):
        o = order[k][0]
        at = pl.ds(pl.multiple_of(r * caps[o], 16), caps[o])
        return pltpu.make_async_remote_copy(
            src_ref=bufs[o].at[at],
            dst_ref=Gs[o].at[m, at],
            send_sem=dsend.at[k],
            recv_sem=drecv.at[k],
            device_id=(peer_of(s, r, 1), m),
            device_id_type=MESH,
        )

    def rows_of(k):
        o, r, n = order[k]
        return r * caps[o], n * caps[o]

    def landed(k, ref):
        start, rows = rows_of(k)
        if start == 0:
            start, rows = caps[order[k][0]], rows - caps[order[k][0]]
        return whole(ref.at[pl.ds(start, rows)], dsend.at[k], drecv.at[k])

    def scatter(k):
        o, r, n = order[k]
        start, rows = rows_of(k)
        row = lax.broadcasted_iota(I32, (rows, TOK), 0) + (o * spans[0] + start)
        pick = (row == drow[...]).astype(F32).astype(BF)
        got = jnp.dot(pick, tok_ref[...], preferred_element_type=F32).astype(BF)
        bufs[o][start:start + rows] = got
        if r == 0:
            Gs[o][m, 0:caps[o]] = got[0:caps[o]]

        def send(at, carry):
            block_copy(k, at).start()
            return carry

        lax.fori_loop(max(r, 1), r + n, send, 0)

    order = [(o, r, n) for o in range(2) for r, n in parts[o]]
    scattered = iter(range(len(order)))

    def scatter_next(count):
        for _, k in zip(range(count), scattered):
            scatter(k)

    loads[3].wait()
    scatter_next(5)

    def ready(t):
        landed(t, Gs[order[t][0]].at[m]).wait_recv()

    def project(k):
        o, r, n = order[k]
        start, size = rows_of(k)
        if k == 0:
            loads[0].wait()
            loads[1].wait()
        cap = caps[o]
        rows = jnp.concatenate([Gs[o][i, start:start + size] for i in range(NMP)], axis=1)
        query = jnp.dot(rows, wq[...], preferred_element_type=F32).astype(BF)
        value = jnp.dot(rows, wv[...], preferred_element_type=F32).astype(BF)
        for j in range(n):
            at = pl.ds(pl.multiple_of(peer_of(s, r + j, -1) * cap, 16), cap)
            qs[o][at] = query[j * cap:(j + 1) * cap]
            for h in range(2):
                vs[o][at, h * 256:h * 256 + HD] = value[j * cap:(j + 1) * cap, h * HD:(h + 1) * HD]

    def tell_counts():
        cnt[0] = lax.dot_general(
            jnp.ones((8, TOK), BF), onehot[...], (((1,), (1,)), ((), ())),
            preferred_element_type=F32,
        )

        def send(r, carry):
            pltpu.make_async_remote_copy(
                src_ref=cnt.at[0], dst_ref=cnt.at[r], send_sem=csend, recv_sem=crecv,
                device_id=(peer_of(s, r, 1), m), device_id_type=MESH,
            ).start()
            return carry

        lax.fori_loop(1, NSEQ, send, 0)

    def counts():
        return whole(cnt.at[pl.ds(1, NSEQ - 1)], csend, crecv)

    def mark(o):
        have = jnp.where(rank == NSEQ * o + s, cnt[:, 0, :], 0.0)
        haves[o][...] = jnp.broadcast_to(jnp.sum(have, axis=1, keepdims=True), (NSEQ, HD))
        place = lax.broadcasted_iota(I32, (caps[o], HD), 0).astype(F32)

        def block(r, carry):
            at = pl.ds(pl.multiple_of(peer_of(s, r, -1) * caps[o], 16), caps[o])
            held = (place < haves[o][pl.ds(r, 1), :]).astype(F32).astype(BF)
            for h in range(2):
                vs[o][at, h * 256 + HD:(h + 1) * 256] = held
            return carry

        lax.fori_loop(0, NSEQ, block, 0)

    def columns():
        for b in range(TOK // BLK):
            at = slice(b * BLK, (b + 1) * BLK)
            dcol[at, :] = column(drow[:, at].astype(F32), BLK).astype(I32)

    def attend(o, i):
        lo, hi = i * BLK, (i + 1) * BLK
        dims = (((1,), (1,)), ((), ()))
        below = i0 >= i1
        for h in range(2):
            lanes = slice(h * HD, (h + 1) * HD)
            wide = slice(h * 256, (h + 1) * 256)
            query = qs[o][lo:hi, lanes]
            near = lax.dot_general(query, query, dims, preferred_element_type=F32) * FOLD
            near = jnp.where(below, near, NEG)
            top = jnp.max(near, axis=1, keepdims=True)
            if i:
                past = lax.dot_general(
                    query, qs[o][0:lo, lanes], dims, preferred_element_type=F32
                ) * FOLD
                top = jnp.maximum(top, jnp.max(past, axis=1, keepdims=True))
                got = jnp.dot(
                    jnp.exp2(past - top).astype(BF), vs[o][0:lo, wide],
                    preferred_element_type=F32,
                )
            expo = jnp.exp2(near - top).astype(BF)
            last = jnp.dot(expo, vs[o][lo:hi, wide], preferred_element_type=F32)
            got = got + last if i else last
            total = jnp.maximum(got[:, HD:], 0.5)
            atts[o][lo:hi, lanes] = (got[:, :HD] / total).astype(BF)

    def give_back(o, first, last):
        def send(at, carry):
            src = first + (at - first + s) % (last - first)
            r = slot_of(s, src)
            rows = pl.ds(pl.multiple_of(src * caps[o], 16), caps[o])

            @pl.when(src != s)
            def _():
                pltpu.make_async_remote_copy(
                    src_ref=atts[o].at[rows],
                    dst_ref=backs[o].at[pl.ds(pl.multiple_of(r * caps[o], 16), caps[o])],
                    send_sem=bsend.at[o],
                    recv_sem=brecv.at[o],
                    device_id=(src, m),
                    device_id_type=MESH,
                ).start()

            return carry

        lax.fori_loop(first, last, send, 0)

    def keep(o):
        backs[o][0:caps[o]] = atts[o][pl.ds(pl.multiple_of(s * caps[o], 16), caps[o])]

    def returned(o):
        ref = backs[o].at[pl.ds(caps[o], (NSEQ - 1) * caps[o])]
        return whole(ref, bsend.at[o], brecv.at[o])

    def pairs(o):
        half = spans[o] // BLK // 2
        ends = [(i + 1) * BLK // caps[o] for i in range(2 * half)]
        for i in range(half):
            yield i, ((ends[i - 1] if i else 0, ends[i]), (ends[i + half - 1], ends[i + half]))

    def attend_pair(o, i):
        half = spans[o] // BLK // 2
        for at, (first, last) in zip((i, i + half), dict(pairs(o))[i]):
            attend(o, at)
        for first, last in dict(pairs(o))[i]:
            give_back(o, first, last)
        if i == half - 1:
            keep(o)

    ring = Ring([(Gs[order[k][0]], *rows_of(k)) for k in range(len(order))], s, m, ssem1, rsem1)

    def open_(k):
        ready(k)
        ring.own(k)

    def close(k):
        ring.shared(k)
        project(k)

    first, n = len(parts[0]), len(order)
    half = spans[0] // BLK // 2
    for t in range(n + 3):
        if t < n:
            open_(t)
        scatter_next(2)
        if t == 2:
            tell_counts()
        if 3 <= t:
            close(t - 3)
        if 2 <= t < n + 2:
            ring.across(t - 2)
        if 1 <= t < n + 1:
            ring.near(t - 1)
        if t == first + 2:
            counts().wait_recv()
            mark(0)
            for i in range(half - 1):
                attend_pair(0, i)
        if t == first + 3:
            attend_pair(0, half - 1)
            mark(1)
    for i in range(spans[1] // BLK // 2):
        attend_pair(1, i)

    loads[2].wait()

    def wcopy(i, block, to):
        return pltpu.make_async_remote_copy(
            src_ref=wo.at[:, pl.ds(pl.multiple_of(to * 256, 256), 256)],
            dst_ref=wcol.at[block],
            send_sem=wsend.at[i],
            recv_sem=wrecv.at[i],
            device_id=(s, to),
            device_id_type=MESH,
        )

    for i in range(1, NMP):
        wcopy(i, m, lax.rem(m + i, NMP)).start()
    wcol[m] = wo[:, pl.ds(pl.multiple_of(m * 256, 256), 256)]

    def unpick(k, o):
        at = dcol[k * ROWS:(k + 1) * ROWS, :]
        col = lax.broadcasted_iota(I32, (ROWS, spans[o]), 1) + o * spans[0]
        pick = (col == at).astype(F32).astype(BF)
        got = jnp.dot(pick, backs[o][...], preferred_element_type=F32).astype(BF)
        at = slice(k * ROWS, (k + 1) * ROWS)
        G2[m, at] = got if o == 0 else got + G2[m, at]

    n = TOK // ROWS
    columns()
    returned(0).wait_recv()
    for k in range(n):
        unpick(k, 0)
    returned(1).wait_recv()

    def mix(k):
        if k == 0:
            for i in range(1, NMP):
                wcopy(i, lax.rem(m + NMP - i, NMP), lax.rem(m + i, NMP)).wait_recv()
        rows = jnp.concatenate(
            [G2[i, k * ROWS:(k + 1) * ROWS] for i in range(NMP)], axis=1
        )
        w = wcol[...].reshape(NMP * 256, 256)
        got = jnp.dot(rows, w, preferred_element_type=F32)
        out_ref[k * ROWS:(k + 1) * ROWS] = got.astype(BF)

    ring2 = Ring([(G2, k * ROWS, ROWS) for k in range(n)], s, m, ssem2, rsem2)
    def send_own(k):
        if k < n:
            unpick(k, 1)
            ring2.own(k)

    for k in range(AHEAD):
        send_own(k)
    for t in range(1, n + 3):
        send_own(t + AHEAD - 1)
        if 3 <= t:
            ring2.shared(t - 3)
            mix(t - 3)
        if 2 <= t < n + 2:
            ring2.across(t - 2)
        if 1 <= t < n + 1:
            ring2.near(t - 1)

    ring.drain()
    ring2.drain()
    for k in range(len(order)):
        landed(k, bufs[order[k][0]]).wait_send()
    counts().wait_send()
    for o in range(2):
        returned(o).wait_send()
    for i in range(1, NMP):
        wcopy(i, m, lax.rem(m + i, NMP)).wait_send()


def layer(tokens, ids, w_query, w_value, w_out, caps, parts, cid):
    vmem = pl.BlockSpec(memory_space=pltpu.VMEM)
    hbm = pl.BlockSpec(memory_space=pl.ANY)
    dma = pltpu.SemaphoreType.DMA
    spans = (NSEQ * caps[0], NSEQ * caps[1])
    chunks, total = TOK // ROWS, sum(len(one) for one in parts)
    G = [pltpu.VMEM((NMP, span, 256), BF) for span in spans]
    flat = [pltpu.VMEM((span, 256), BF) for span in spans]
    return pl.pallas_call(
        functools.partial(layer_kernel, caps=caps, parts=parts),
        out_shape=jax.ShapeDtypeStruct((TOK, 256), BF),
        in_specs=[vmem] + [hbm] * 4,
        out_specs=vmem,
        scratch_shapes=[
            pltpu.VMEM((TOK, 256), BF),
            pltpu.VMEM((2048, 256), BF),
            pltpu.VMEM((2048, 256), BF),
            pltpu.VMEM((256, 2048), BF),
            pltpu.VMEM((NMP, 256, 256), BF),
            *flat,
            *G,
            *flat,
            *[pltpu.VMEM((span, 512), BF) for span in spans],
            *[pltpu.VMEM((NSEQ, HD), F32)] * 2,
            *flat,
            *flat,
            pltpu.VMEM((NMP, TOK, 256), BF),
            pltpu.VMEM((NSEQ, 8, 128), F32),
            pltpu.VMEM((128, TOK), BF),
            pltpu.VMEM((1, TOK), I32),
            pltpu.VMEM((TOK, 1), I32),
            dma((4,)),
            dma((8, total)), dma((8, total)),
            dma((8, chunks)), dma((8, chunks)),
            dma((total,)), dma((total,)),
            dma, dma,
            dma((2,)), dma((2,)),
            dma((NMP,)), dma((NMP,)),
        ],
        compiler_params=pltpu.CompilerParams(
            collective_id=cid, has_side_effects=True, vmem_limit_bytes=60 * 1024 * 1024
        ),
        name="layer",
    )(ids, tokens, w_query, w_value, w_out)


def shards(tokens, cluster_ids, w_query, w_value, w_out):
    ids = cluster_ids.reshape(1, TOK)
    return layer(tokens, ids, w_query, w_value, w_out, (CAP, CAP), (FIRST, SECOND), 1)


def solution(mesh):
    return jax.shard_map(
        shards,
        mesh=mesh,
        in_specs=(P("seq", "mp"), P("seq", None), P(None, "mp"), P(None, "mp"), P("mp", None)),
        out_specs=P("seq", "mp"),
        check_vma=False,
    )
```

```python
import functools

import jax
import jax.numpy as jnp
import numpy as np
from jax import lax
from jax.experimental import pallas as pl
from jax.experimental.pallas import tpu as pltpu
from jax.sharding import PartitionSpec as P

HD = 128
CAP = 48
NZ, NY, NX = 8, 4, 4
NSEQ = NZ * NY
NMP = 2 * NX
TOK = 1536
BLK = 256
ROWS = 384
AHEAD = 1
FIRST = ((0, 4), (8, 8), (16, 8), (24, 8), (4, 4))
SECOND = ((8, 8), (16, 8), (24, 8), (0, 8))
NEG = -1e30
MESH = pl.DeviceIdType.MESH
BF = jnp.bfloat16
F32 = jnp.float32
I32 = jnp.int32
FOLD = np.float32(1.4426950408889634 / np.sqrt(128.0))


def peer_of(s, r, sign):
    g, hi, dy = r // 8, (r // 4) % 2, r % 4
    minus = jnp.where(g == 0, 4, NZ - g)
    dz = jnp.where(hi == 0, g, minus)
    z, y = s // NY, s % NY
    return ((z + sign * dz + NZ) % NZ) * NY + (y + sign * dy + NY) % NY


def rank_of(cluster):
    return (cluster & 1) * NSEQ + (cluster >> 1)


def slot_of(s, src):
    dz = (s // NY - src // NY + NZ) % NZ
    hi = dz // 4
    g = (1 - hi) * dz + hi * ((NZ - dz) % 4)
    return g * 8 + hi * 4 + (s % NY - src % NY + NY) % NY


def first_row(rank, s, caps):
    z, y = s // NY, s % NY
    owner, o = rank & (NSEQ - 1), rank >> 5
    dz = ((owner >> 2) - z) & (NZ - 1)
    dy = ((owner & 3) - y) & (NY - 1)
    hi = dz >> 2
    g = jnp.where(hi == 1, (NZ - dz) & 3, dz)
    r = g * 8 + hi * 4 + dy
    return jnp.where(o == 0, r * caps[0], NSEQ * caps[0] + r * caps[1])


class Ring:
    def __init__(self, chunks, s, m, ssem, rsem):
        self.chunks, self.s, self.m = chunks, s, m
        self.ssem, self.rsem = ssem, rsem
        x, c = m // 2, m % 2
        self.right = ((x + 1) % NX) * 2 + c
        self.left = ((x + NX - 1) % NX) * 2 + c
        self.far = ((x + 2) % NX) * 2 + c
        self.sib = x * 2 + 1 - c

    def _copy(self, kind, k, block, to, half=None):
        G, start, rows = self.chunks[k]
        if half is not None:
            rows = rows // 2
            start = start + half * rows
        ref = G.at[block, pl.ds(start, rows)]
        return pltpu.make_async_remote_copy(
            src_ref=ref,
            dst_ref=ref,
            send_sem=self.ssem.at[kind, k],
            recv_sem=self.rsem.at[kind, k],
            device_id=(self.s, to),
            device_id_type=MESH,
        )

    def send(self, i, k):
        block, to, half = (
            (self.m, self.right, None),
            (self.m, self.left, None),
            (self.m, self.sib, None),
            (self.left, self.right, 0),
            (self.right, self.left, 1),
            (self.left, self.sib, None),
            (self.right, self.sib, None),
            (self.far, self.sib, None),
        )[i]
        return self._copy(i, k, block, to, half)

    def arrival(self, i, k):
        other = lambda block: (block // 2) * 2 + 1 - block % 2
        block, half = (
            (self.left, None),
            (self.right, None),
            (self.sib, None),
            (self.far, 0),
            (self.far, 1),
            (other(self.left), None),
            (other(self.right), None),
            (other(self.far), None),
        )[i]
        return self._copy(i, k, block, self.sib, half)

    def own(self, k):
        for i in (0, 1, 2):
            self.send(i, k).start()

    def near(self, k):
        self.arrival(0, k).wait_recv()
        self.send(3, k).start()
        self.send(5, k).start()
        self.arrival(1, k).wait_recv()
        self.send(4, k).start()
        self.send(6, k).start()

    def across(self, k):
        self.arrival(3, k).wait_recv()
        self.arrival(4, k).wait_recv()
        self.send(7, k).start()

    def shared(self, k):
        for i in (2, 5, 6, 7):
            self.arrival(i, k).wait_recv()

    def drain(self):
        for k in range(len(self.chunks)):
            for i in range(8):
                self.send(i, k).wait_send()


def greet(s, m, mp_peers):
    barrier = pltpu.get_barrier_semaphore()

    def hello(r, carry):
        pl.semaphore_signal(
            barrier, inc=1, device_id=(peer_of(s, r, 1), m), device_id_type=MESH
        )
        return carry

    lax.fori_loop(1, NSEQ, hello, 0)
    for i in range(1, 1 + mp_peers):
        pl.semaphore_signal(
            barrier, inc=1, device_id=(s, lax.rem(m + i, NMP)), device_id_type=MESH
        )
    return barrier


def column(row, n):
    eye = lax.broadcasted_iota(I32, (n, n), 0) == lax.broadcasted_iota(I32, (n, n), 1)
    return jnp.sum(jnp.where(eye, row, 0.0), axis=1, keepdims=True)


def layer_kernel(
    row_ref, tok_hbm, wq_hbm, wv_hbm, wo_hbm,
    out_hbm,
    out_ref, osem, tok_ref, wq, wv, wo, wcol, buf0, buf1, G0, G1, q0, q1, v0, v1, have0, have1,
    att0, att1, back0, back1, G2, cnt, onehot, drow, dcol,
    lsem, ssem1, rsem1, ssem2, rsem2, dsend, drecv, csend, crecv,
    bsend, brecv, wsend, wrecv,
    *, caps, parts,
):
    s, m = lax.axis_index("seq"), lax.axis_index("mp")
    bufs, Gs, qs, vs = (buf0, buf1), (G0, G1), (q0, q1), (v0, v1)
    haves, atts, backs = (have0, have1), (att0, att1), (back0, back1)
    spans = (NSEQ * caps[0], NSEQ * caps[1])

    loads = [
        pltpu.make_async_copy(a, b, lsem.at[i])
        for i, (a, b) in enumerate(
            ((wq_hbm, wq), (wv_hbm, wv), (wo_hbm, wo), (tok_hbm, tok_ref))
        )
    ]
    barrier = greet(s, m, NMP - 1)
    for i in (3, 0, 1, 2):
        loads[i].start()

    i0 = lax.broadcasted_iota(I32, (BLK, BLK), 0)
    i1 = lax.broadcasted_iota(I32, (BLK, BLK), 1)
    upper = (i0 < i1).astype(F32).astype(BF)
    onehot[...] = (
        lax.broadcasted_iota(I32, (128, TOK), 0) == row_ref[...]
    ).astype(F32).astype(BF)
    rank = rank_of(lax.broadcasted_iota(I32, (1, 128), 1))
    seen = first_row(rank_of(lax.broadcasted_iota(I32, (128, 1), 0)), s, caps).astype(F32)
    for b in range(TOK // BLK):
        part = onehot[:, b * BLK:(b + 1) * BLK]
        wide = part.astype(F32)
        ahead = jnp.dot(part, upper, preferred_element_type=F32) + seen
        drow[:, b * BLK:(b + 1) * BLK] = jnp.sum(ahead * wide, axis=0, keepdims=True).astype(I32)
        seen = seen + jnp.sum(wide, axis=1, keepdims=True)
    pl.semaphore_wait(barrier, NSEQ - 1 + NMP - 1)

    def whole(ref, sem_s, sem_r):
        return pltpu.make_async_remote_copy(
            src_ref=ref, dst_ref=ref, send_sem=sem_s, recv_sem=sem_r,
            device_id=(s, m), device_id_type=MESH,
        )

    def block_copy(k, r):
        o = order[k][0]
        at = pl.ds(pl.multiple_of(r * caps[o], 16), caps[o])
        return pltpu.make_async_remote_copy(
            src_ref=bufs[o].at[at],
            dst_ref=Gs[o].at[m, at],
            send_sem=dsend.at[k],
            recv_sem=drecv.at[k],
            device_id=(peer_of(s, r, 1), m),
            device_id_type=MESH,
        )

    def rows_of(k):
        o, r, n = order[k]
        return r * caps[o], n * caps[o]

    def landed(k, ref):
        start, rows = rows_of(k)
        if start == 0:
            start, rows = caps[order[k][0]], rows - caps[order[k][0]]
        return whole(ref.at[pl.ds(start, rows)], dsend.at[k], drecv.at[k])

    def scatter(k):
        o, r, n = order[k]
        start, rows = rows_of(k)
        row = lax.broadcasted_iota(I32, (rows, TOK), 0) + (o * spans[0] + start)
        pick = (row == drow[...]).astype(F32).astype(BF)
        got = jnp.dot(pick, tok_ref[...], preferred_element_type=F32).astype(BF)
        bufs[o][start:start + rows] = got
        if r == 0:
            Gs[o][m, 0:caps[o]] = got[0:caps[o]]

        def send(at, carry):
            block_copy(k, at).start()
            return carry

        lax.fori_loop(max(r, 1), r + n, send, 0)

    order = [(o, r, n) for o in range(2) for r, n in parts[o]]
    scattered = iter(range(len(order)))

    def scatter_next(count):
        for _, k in zip(range(count), scattered):
            scatter(k)

    loads[3].wait()
    scatter_next(5)

    def ready(t):
        landed(t, Gs[order[t][0]].at[m]).wait_recv()

    def project(k):
        o, r, n = order[k]
        start, size = rows_of(k)
        if k == 0:
            loads[0].wait()
            loads[1].wait()
        cap = caps[o]
        rows = jnp.concatenate([Gs[o][i, start:start + size] for i in range(NMP)], axis=1)
        query = jnp.dot(rows, wq[...], preferred_element_type=F32).astype(BF)
        value = jnp.dot(rows, wv[...], preferred_element_type=F32).astype(BF)
        for j in range(n):
            at = pl.ds(pl.multiple_of(peer_of(s, r + j, -1) * cap, 16), cap)
            qs[o][at] = query[j * cap:(j + 1) * cap]
            for h in range(2):
                vs[o][at, h * 256:h * 256 + HD] = value[j * cap:(j + 1) * cap, h * HD:(h + 1) * HD]

    def tell_counts():
        cnt[0] = lax.dot_general(
            jnp.ones((8, TOK), BF), onehot[...], (((1,), (1,)), ((), ())),
            preferred_element_type=F32,
        )

        def send(r, carry):
            pltpu.make_async_remote_copy(
                src_ref=cnt.at[0], dst_ref=cnt.at[r], send_sem=csend, recv_sem=crecv,
                device_id=(peer_of(s, r, 1), m), device_id_type=MESH,
            ).start()
            return carry

        lax.fori_loop(1, NSEQ, send, 0)

    def counts():
        return whole(cnt.at[pl.ds(1, NSEQ - 1)], csend, crecv)

    def mark(o):
        have = jnp.where(rank == NSEQ * o + s, cnt[:, 0, :], 0.0)
        haves[o][...] = jnp.broadcast_to(jnp.sum(have, axis=1, keepdims=True), (NSEQ, HD))
        place = lax.broadcasted_iota(I32, (caps[o], HD), 0).astype(F32)

        def block(r, carry):
            at = pl.ds(pl.multiple_of(peer_of(s, r, -1) * caps[o], 16), caps[o])
            held = (place < haves[o][pl.ds(r, 1), :]).astype(F32).astype(BF)
            for h in range(2):
                vs[o][at, h * 256 + HD:(h + 1) * 256] = held
            return carry

        lax.fori_loop(0, NSEQ, block, 0)

    def columns():
        for b in range(TOK // BLK):
            at = slice(b * BLK, (b + 1) * BLK)
            dcol[at, :] = column(drow[:, at].astype(F32), BLK).astype(I32)

    def attend(o, i):
        lo, hi = i * BLK, (i + 1) * BLK
        dims = (((1,), (1,)), ((), ()))
        below = i0 >= i1
        for h in range(2):
            lanes = slice(h * HD, (h + 1) * HD)
            wide = slice(h * 256, (h + 1) * 256)
            query = qs[o][lo:hi, lanes]
            near = lax.dot_general(query, query, dims, preferred_element_type=F32) * FOLD
            near = jnp.where(below, near, NEG)
            top = jnp.max(near, axis=1, keepdims=True)
            if i:
                past = lax.dot_general(
                    query, qs[o][0:lo, lanes], dims, preferred_element_type=F32
                ) * FOLD
                top = jnp.maximum(top, jnp.max(past, axis=1, keepdims=True))
                got = jnp.dot(
                    jnp.exp2(past - top).astype(BF), vs[o][0:lo, wide],
                    preferred_element_type=F32,
                )
            expo = jnp.exp2(near - top).astype(BF)
            last = jnp.dot(expo, vs[o][lo:hi, wide], preferred_element_type=F32)
            got = got + last if i else last
            total = jnp.maximum(got[:, HD:], 0.5)
            atts[o][lo:hi, lanes] = (got[:, :HD] / total).astype(BF)

    def give_back(o, first, last):
        def send(at, carry):
            src = first + (at - first + s) % (last - first)
            r = slot_of(s, src)
            rows = pl.ds(pl.multiple_of(src * caps[o], 16), caps[o])

            @pl.when(src != s)
            def _():
                pltpu.make_async_remote_copy(
                    src_ref=atts[o].at[rows],
                    dst_ref=backs[o].at[pl.ds(pl.multiple_of(r * caps[o], 16), caps[o])],
                    send_sem=bsend.at[o],
                    recv_sem=brecv.at[o],
                    device_id=(src, m),
                    device_id_type=MESH,
                ).start()

            return carry

        lax.fori_loop(first, last, send, 0)

    def keep(o):
        backs[o][0:caps[o]] = atts[o][pl.ds(pl.multiple_of(s * caps[o], 16), caps[o])]

    def returned(o):
        ref = backs[o].at[pl.ds(caps[o], (NSEQ - 1) * caps[o])]
        return whole(ref, bsend.at[o], brecv.at[o])

    def pairs(o):
        half = spans[o] // BLK // 2
        ends = [(i + 1) * BLK // caps[o] for i in range(2 * half)]
        for i in range(half):
            yield i, ((ends[i - 1] if i else 0, ends[i]), (ends[i + half - 1], ends[i + half]))

    def attend_pair(o, i):
        half = spans[o] // BLK // 2
        for at, (first, last) in zip((i, i + half), dict(pairs(o))[i]):
            attend(o, at)
        for first, last in dict(pairs(o))[i]:
            give_back(o, first, last)
        if i == half - 1:
            keep(o)

    ring = Ring([(Gs[order[k][0]], *rows_of(k)) for k in range(len(order))], s, m, ssem1, rsem1)

    def open_(k):
        ready(k)
        ring.own(k)

    def close(k):
        ring.shared(k)
        project(k)

    first, n = len(parts[0]), len(order)
    half = spans[0] // BLK // 2
    for t in range(n + 3):
        if t < n:
            open_(t)
        scatter_next(2)
        if t == 2:
            tell_counts()
        if 3 <= t:
            close(t - 3)
        if 2 <= t < n + 2:
            ring.across(t - 2)
        if 1 <= t < n + 1:
            ring.near(t - 1)
        if t == first + 2:
            counts().wait_recv()
            mark(0)
            for i in range(half - 1):
                attend_pair(0, i)
        if t == first + 3:
            attend_pair(0, half - 1)
            mark(1)
    for i in range(spans[1] // BLK // 2):
        attend_pair(1, i)

    loads[2].wait()

    def wcopy(i, block, to):
        return pltpu.make_async_remote_copy(
            src_ref=wo.at[:, pl.ds(pl.multiple_of(to * 256, 256), 256)],
            dst_ref=wcol.at[block],
            send_sem=wsend.at[i],
            recv_sem=wrecv.at[i],
            device_id=(s, to),
            device_id_type=MESH,
        )

    for i in range(1, NMP):
        wcopy(i, m, lax.rem(m + i, NMP)).start()
    wcol[m] = wo[:, pl.ds(pl.multiple_of(m * 256, 256), 256)]

    def unpick(k, o):
        at = dcol[k * ROWS:(k + 1) * ROWS, :]
        col = lax.broadcasted_iota(I32, (ROWS, spans[o]), 1) + o * spans[0]
        pick = (col == at).astype(F32).astype(BF)
        got = jnp.dot(pick, backs[o][...], preferred_element_type=F32).astype(BF)
        at = slice(k * ROWS, (k + 1) * ROWS)
        G2[m, at] = got if o == 0 else got + G2[m, at]

    n = TOK // ROWS
    columns()
    returned(0).wait_recv()
    for k in range(n):
        unpick(k, 0)
    returned(1).wait_recv()

    def store(k):
        at = pl.ds(k * ROWS, ROWS)
        return pltpu.make_async_copy(out_ref.at[at], out_hbm.at[at], osem.at[k])

    def mix(k):
        if k == 0:
            for i in range(1, NMP):
                wcopy(i, lax.rem(m + NMP - i, NMP), lax.rem(m + i, NMP)).wait_recv()
        rows = jnp.concatenate(
            [G2[i, k * ROWS:(k + 1) * ROWS] for i in range(NMP)], axis=1
        )
        w = wcol[...].reshape(NMP * 256, 256)
        got = jnp.dot(rows, w, preferred_element_type=F32)
        out_ref[k * ROWS:(k + 1) * ROWS] = got.astype(BF)
        store(k).start()

    ring2 = Ring([(G2, k * ROWS, ROWS) for k in range(n)], s, m, ssem2, rsem2)
    def send_own(k):
        if k < n:
            unpick(k, 1)
            ring2.own(k)

    for k in range(AHEAD):
        send_own(k)
    for t in range(1, n + 3):
        send_own(t + AHEAD - 1)
        if 3 <= t:
            ring2.shared(t - 3)
            mix(t - 3)
        if 2 <= t < n + 2:
            ring2.across(t - 2)
        if 1 <= t < n + 1:
            ring2.near(t - 1)

    for k in range(n):
        store(k).wait()
    ring.drain()
    ring2.drain()
    for k in range(len(order)):
        landed(k, bufs[order[k][0]]).wait_send()
    counts().wait_send()
    for o in range(2):
        returned(o).wait_send()
    for i in range(1, NMP):
        wcopy(i, m, lax.rem(m + i, NMP)).wait_send()


def layer(tokens, ids, w_query, w_value, w_out, caps, parts, cid):
    vmem = pl.BlockSpec(memory_space=pltpu.VMEM)
    hbm = pl.BlockSpec(memory_space=pl.ANY)
    dma = pltpu.SemaphoreType.DMA
    spans = (NSEQ * caps[0], NSEQ * caps[1])
    chunks, total = TOK // ROWS, sum(len(one) for one in parts)
    G = [pltpu.VMEM((NMP, span, 256), BF) for span in spans]
    flat = [pltpu.VMEM((span, 256), BF) for span in spans]
    return pl.pallas_call(
        functools.partial(layer_kernel, caps=caps, parts=parts),
        out_shape=jax.ShapeDtypeStruct((TOK, 256), BF),
        in_specs=[vmem] + [hbm] * 4,
        out_specs=hbm,
        scratch_shapes=[
            pltpu.VMEM((TOK, 256), BF),
            dma((chunks,)),
            pltpu.VMEM((TOK, 256), BF),
            pltpu.VMEM((2048, 256), BF),
            pltpu.VMEM((2048, 256), BF),
            pltpu.VMEM((256, 2048), BF),
            pltpu.VMEM((NMP, 256, 256), BF),
            *flat,
            *G,
            *flat,
            *[pltpu.VMEM((span, 512), BF) for span in spans],
            *[pltpu.VMEM((NSEQ, HD), F32)] * 2,
            *flat,
            *flat,
            pltpu.VMEM((NMP, TOK, 256), BF),
            pltpu.VMEM((NSEQ, 8, 128), F32),
            pltpu.VMEM((128, TOK), BF),
            pltpu.VMEM((1, TOK), I32),
            pltpu.VMEM((TOK, 1), I32),
            dma((4,)),
            dma((8, total)), dma((8, total)),
            dma((8, chunks)), dma((8, chunks)),
            dma((total,)), dma((total,)),
            dma, dma,
            dma((2,)), dma((2,)),
            dma((NMP,)), dma((NMP,)),
        ],
        compiler_params=pltpu.CompilerParams(
            collective_id=cid, has_side_effects=True, vmem_limit_bytes=60 * 1024 * 1024
        ),
        name="layer",
    )(ids, tokens, w_query, w_value, w_out)


def shards(tokens, cluster_ids, w_query, w_value, w_out):
    ids = cluster_ids.reshape(1, TOK)
    return layer(tokens, ids, w_query, w_value, w_out, (CAP, CAP), (FIRST, SECOND), 1)


def solution(mesh):
    return jax.shard_map(
        shards,
        mesh=mesh,
        in_specs=(P("seq", "mp"), P("seq", None), P(None, "mp"), P(None, "mp"), P("mp", None)),
        out_specs=P("seq", "mp"),
        check_vma=False,
    )
```
